128 devices in a mesh: role: 2 (over core), dev: 64 (over z, y, x).
Axes of the slice: x: 4, y: 4, z: 4, core: 2. Of those that a mesh axis runs over, the one named last changes fastest.
Arguments:
- hidden_in: bfloat16 [512, 7168], P('dev'), may hold values from -250 to 250
- expert_ids: int32 [512, 8], P('dev'), may hold values from 0 to 15, all different within a row
- gate_values: float32 [512, 8], P('dev'), may hold values from 0.2 to 2
- ffn_gain: float32 [7168], replicated, may hold values from 0.25 to 1.75
- w_gate: bfloat16 [7168, 32768], P(None, 'dev'), may hold values from -0.0625 to 0.0625
- w_up: bfloat16 [7168, 32768], P(None, 'dev'), may hold values from -0.0625 to 0.0625
- w_down: bfloat16 [32768, 7168], P('dev'), may hold values from -0.125 to 0.125
- attn_gain: float32 [7168], replicated, may hold values from 0.25 to 1.75
- w_latent: bfloat16 [7168, 576], P('dev'), may hold values from -2 to 2
- kv_gain: float32 [512], replicated, may hold values from 0.25 to 1.75
- queries: bfloat16 [512, 128, 576], P('dev'), may hold values from -13 to 13
- cache: bfloat16 [512, 256, 576], P('dev'), may hold values from -6 to 6
- lengths: int32 [512], P('dev'), may hold values from 2 to 256, as said below
Outputs:
- new_latent: bfloat16 [512, 576], P('dev')
- context: bfloat16 [512, 128, 512], P('dev', 'role')
The draws below stay inside these ranges and needn't reach their ends.
Inputs may be any that keep to these rules, and one draw needn't show every extreme that they name: `lengths`: one request has exactly 256 live positions.
All inputs are finite; a program needn't handle non-finite values.
Results may differ from the reference program's by a relative error of at most 0.0063.
Values may be sent and summed in bfloat16 or wider, within the bound.
A program may use at most 128 MiB of HBM per device.

```python
import math
import jax
import jax.numpy as jnp
from jax import lax

D = 7168
FF = 2048
HEADS = 128
LATENT = 512
TOP = 8
EXPERTS = 16
ROW_DEV = 8
CACHE = 256
KVW = 576
SPLIT = 4
FF_DEV = 512
ROWS = 512
N_DEV = 64


def draw_cache(key, part):
    key = jax.random.fold_in(key, 5)
    noise_field = jax.random.truncated_normal(key, -6.0, 6.0, (ROWS, CACHE, KVW), jnp.float32)
    return noise_field.astype(jnp.bfloat16)


def draw_queries(key, part):
    key = jax.random.fold_in(key, 6)
    noise_field = jax.random.truncated_normal(key, -6.0, 6.0, (ROWS, HEADS, KVW), jnp.float32)
    return noise_field.astype(jnp.bfloat16)


def draw_hidden_in(key, part):
    key = jax.random.fold_in(key, 1)
    row_key, column_key, noise_key = jax.random.split(key, 3)
    row_scale = jnp.exp(jax.random.uniform(row_key, (ROWS, 1), jnp.float32, 0.0, 2.302585))
    column_scale = jnp.exp(jax.random.uniform(column_key, (1, D), jnp.float32, 0.0, 2.302585))
    noise_field = jax.random.truncated_normal(noise_key, -6.0, 6.0, (ROWS, D), jnp.float32)
    return (noise_field * row_scale * column_scale * 0.25).astype(jnp.bfloat16)


def draw_w_latent(key, part):
    key = jax.random.fold_in(key, 2)
    column_key, noise_key = jax.random.split(key, 2)
    column_scale = jnp.exp(jax.random.uniform(column_key, (1, KVW), jnp.float32, -1.2039728, 1.0986123))
    noise_field = jax.random.truncated_normal(noise_key, -6.0, 6.0, (D, KVW), jnp.float32)
    return (noise_field * column_scale * (1.0 / D) ** 0.5).astype(jnp.bfloat16)


def draw_lengths(key, part):
    key = jax.random.fold_in(key, 4)
    length_key, full_key = jax.random.split(key, 2)
    drawn_lengths = jax.random.randint(length_key, (ROWS,), 2, CACHE + 1)
    full_row = jax.random.randint(full_key, (), 0, ROWS)
    return jnp.where(jnp.arange(ROWS) == full_row, CACHE, drawn_lengths).astype(jnp.int32)


def steps_of(own_key, extent, cuts, smallest, high):
    loudness = 1.0
    for dim, blocks in cuts:
        steps = jax.random.uniform(jax.random.fold_in(jax.random.fold_in(own_key, 6), dim), (blocks,), jnp.float32, smallest / len(cuts), high / len(cuts))
        loudness = loudness * jnp.repeat(jnp.exp(steps), extent[dim] // blocks).reshape((-1,) + (1,) * (len(extent) - 1 - dim))
    return loudness


def picks_of(key, rows, amount, top, lift):
    sequence = jax.random.permutation(jax.random.fold_in(key, 1), amount)
    pull = sequence
    for power in range(3):
        pull = pull * pull // amount
    pull = pull * lift // amount
    lots = jax.random.randint(jax.random.fold_in(key, 2), (rows, amount), 0, 4096) + pull
    sure = jax.random.permutation(jax.random.fold_in(key, 3), rows)[jnp.arange(amount) % rows]
    lots = jnp.where(jnp.arange(rows)[:, None] == sure[None, :], 1 << 14, lots)
    priority = lots * amount + jnp.arange(amount)
    return lax.top_k(priority.astype(jnp.int32), top)[1].astype(jnp.int32)


def gaussian(own_key, dims, width, limit, cuts=(), held_as=jnp.bfloat16):
    result = width * jax.random.normal(own_key, dims, jnp.float32)
    if cuts:
        result = result * steps_of(own_key, dims, cuts, -0.22, 0.18)
    return jnp.clip(result, -limit, limit).astype(held_as)


def setup_inputs(seed: int = 0) -> dict:
    key_list = jax.random.split(jax.random.key(seed), 14)
    return {
        "hidden_in": draw_hidden_in(jax.random.fold_in(key_list[13], 71), 0),
        "expert_ids": picks_of(key_list[1], ROWS, EXPERTS, TOP, 8192),
        "gate_values": jnp.clip(jnp.exp(math.log(2.0) - 2.3025851 * jax.random.uniform(key_list[2], (ROWS, TOP), jnp.float32) ** steps_of(key_list[2], (ROWS, TOP), ((0, 64),), -0.2, 0.2)), 0.2, 2.0),
        "ffn_gain": jnp.clip(1.0 + 0.15 * jax.random.normal(key_list[3], (D,), jnp.float32), 0.25, 1.75),
        "w_gate": gaussian(key_list[4], (D, EXPERTS * FF), D ** -0.5, 0.0625, ((1, 64),)),
        "w_up": gaussian(key_list[5], (D, EXPERTS * FF), D ** -0.5, 0.0625, ((1, 64),)),
        "w_down": gaussian(key_list[6], (EXPERTS * FF, D), FF ** -0.5, 0.125, ((0, 64),)),
        "attn_gain": jnp.clip(1.0 + 0.15 * jax.random.normal(key_list[7], (D,), jnp.float32), 0.25, 1.75),
        "w_latent": draw_w_latent(jax.random.fold_in(key_list[13], 71), 0),
        "kv_gain": jnp.clip(1.0 + 0.15 * jax.random.normal(key_list[9], (LATENT,), jnp.float32), 0.25, 1.75),
        "queries": draw_queries(jax.random.fold_in(key_list[13], 71), 0),
        "cache": draw_cache(jax.random.fold_in(key_list[13], 71), 0),
        "lengths": draw_lengths(jax.random.fold_in(key_list[13], 71), 0),
    }


score_scale = 192.0 ** (-0.5)
norm_eps = 1e-06

def rms_scale(values, gain):
    mean_square = lax.optimization_barrier(jnp.mean(jnp.square(values), axis=-1, keepdims=True))
    return values * lax.rsqrt(mean_square + norm_eps) * gain

def cache_state(query_part, cache_rows, length_rows):
    scores = jnp.einsum('rhc,rlc->rhl', query_part.astype(jnp.float32), cache_rows.astype(jnp.float32)) * score_scale
    live_mask = jnp.arange(cache_rows.shape[1], dtype=jnp.int32)[None, None, :] < length_rows[:, None, None]
    scores = jnp.where(live_mask, scores, -jnp.inf)
    peak_cache = lax.optimization_barrier(jnp.max(scores, axis=2))
    weights = jnp.where(live_mask, jnp.exp(scores - peak_cache[:, :, None]), 0.0).astype(jnp.bfloat16)
    weights = lax.optimization_barrier(weights).astype(jnp.float32)
    weight_sum = lax.optimization_barrier(jnp.sum(weights, axis=2))
    summed = jnp.einsum('rhl,rlc->rhc', weights, cache_rows[:, :, :LATENT].astype(jnp.float32))
    return (peak_cache, weight_sum, summed)

def finish(peak_cache, weight_sum, summed, query_part, latent_rows):
    new_score = jnp.einsum('rhc,rc->rh', query_part.astype(jnp.float32), latent_rows.astype(jnp.float32)) * score_scale
    joint_peak = jnp.maximum(peak_cache, new_score)
    old_scale = jnp.exp(peak_cache - joint_peak)
    new_scale = jnp.exp(new_score - joint_peak)
    values = latent_rows[:, None, :LATENT].astype(jnp.float32)
    merged = (old_scale[:, :, None] * summed + new_scale[:, :, None] * values) / (old_scale * weight_sum + new_scale)[:, :, None]
    return merged.astype(jnp.bfloat16)

def reshape_rows(array):
    return array.reshape((N_DEV, ROW_DEV) + array.shape[1:])

def reference(hidden_in, expert_ids, gate_values, ffn_gain, w_gate, w_up, w_down, attn_gain, w_latent, kv_gain, queries, cache, lengths):
    normed = rms_scale(hidden_in.astype(jnp.float32), ffn_gain).astype(jnp.bfloat16)
    matches = expert_ids[:, :, None] == jnp.arange(EXPERTS, dtype=jnp.int32)[None, None, :]
    table = lax.optimization_barrier(jnp.sum(jnp.where(matches, gate_values[:, :, None], 0.0), axis=1))
    combined = jnp.zeros(hidden_in.shape, jnp.float32)
    for expert in range(EXPERTS):
        first_col = expert * FF
        gate_act = jnp.dot(normed, w_gate[:, first_col:first_col + FF], preferred_element_type=jnp.float32)
        up_act = jnp.dot(normed, w_up[:, first_col:first_col + FF], preferred_element_type=jnp.float32)
        hidden_act = (jax.nn.silu(gate_act) * up_act).astype(jnp.bfloat16)
        output = jnp.zeros(hidden_in.shape, jnp.float32)
        for part_index in range(SPLIT):
            part_start = part_index * FF_DEV
            part_rows = w_down[first_col + part_start:first_col + part_start + FF_DEV]
            partial_out = jnp.dot(hidden_act[:, part_start:part_start + FF_DEV], part_rows, preferred_element_type=jnp.float32)
            output = output + lax.optimization_barrier(partial_out.astype(jnp.bfloat16)).astype(jnp.float32)
        combined = combined + table[:, expert:expert + 1] * output
    residual = lax.optimization_barrier((hidden_in.astype(jnp.float32) + combined).astype(jnp.bfloat16))
    attn_in = rms_scale(residual.astype(jnp.float32), attn_gain).astype(jnp.bfloat16)
    compressed = jnp.dot(attn_in, w_latent, preferred_element_type=jnp.float32)
    content = rms_scale(compressed[:, :LATENT], kv_gain)
    new_latent = jnp.concatenate([content, compressed[:, LATENT:]], axis=1).astype(jnp.bfloat16)

    def per_rows(row_group):
        query_part, cache_rows, length_rows, latent_rows = row_group
        peak_cache, weight_sum, summed = cache_state(query_part, cache_rows, length_rows)
        return finish(peak_cache, weight_sum, summed, query_part, latent_rows)
    context = lax.map(per_rows, (reshape_rows(queries), reshape_rows(cache), reshape_rows(lengths), reshape_rows(new_latent)))
    context = context.reshape(ROWS, HEADS, LATENT)
    return (new_latent, context)
```

```python
import jax
import jax.numpy as jnp
from jax import lax
from jax.experimental import pallas as pl
from jax.experimental.pallas import tpu as pltpu
from jax.sharding import PartitionSpec as P

MESH = pl.DeviceIdType.MESH
F32 = jnp.float32
BF16 = jnp.bfloat16

SCORE_SCALE = 192.0 ** (-0.5)
EPS = 1e-06
D = 7168
SLICE = 1792
FFD = 512
LAT = 512
KVW = 576
EXPERTS = 16
WIDTH = (640, 640, 512)
OFF = (0, 640, 1280)
GATHER = (("x", "y", "z"), ("y", "z", "x"), ("z", "x", "y"))
SCATTER = tuple(order[::-1] for order in GATHER)
DIM = {"z": 0, "x": 1, "y": 2}
LOW_ROWS = 64


def kernel(
    hidden,
    ids,
    gates,
    ffn_gain,
    attn_gain,
    kv_gain,
    lengths,
    w_gate,
    w_up,
    w_down,
    w_latent,
    queries,
    cache,
    new_latent,
    context,
    wg,
    wu,
    wd,
    wl,
    qv,
    cv,
    summed,
    peaks,
    sums,
    xh,
    xe,
    yh,
    ye,
    hid16,
    ga,
    gb,
    gc,
    acc_g,
    acc_u,
    gate_col,
    act,
    oa,
    ob,
    oc,
    rs_bufs,
    att,
    tbuf,
    ebuf,
    send_sems,
    recv_sems,
    load_sems,
):
    role = lax.axis_index("role")
    dev = lax.axis_index("dev")
    z, y, x = dev // 16, lax.rem(dev // 4, 4), lax.rem(dev, 4)
    at = {"z": z, "y": y, "x": x}
    stride = {"z": 16, "y": 4, "x": 1}

    def plus(axis, d):
        return lax.rem(at[axis] + (d + 4), 4)

    def near(axis, d):
        return dev + (plus(axis, d) - at[axis]) * stride[axis]

    count = [0]
    sent = []

    def remote(src, dst, to_dev, to_role=None):
        i = count[0]
        count[0] += 1
        return pltpu.make_async_remote_copy(
            src_ref=src,
            dst_ref=dst,
            send_sem=send_sems.at[i],
            recv_sem=recv_sems.at[i],
            device_id=(role if to_role is None else to_role, to_dev),
            device_id_type=MESH,
        )

    def go(copy):
        copy.start()
        sent.append(copy)
        return copy

    loads = []

    def load(src, dst):
        copy = pltpu.make_async_copy(src, dst, load_sems.at[len(loads)])
        copy.start()
        loads.append(copy)
        return copy

    load_q = load(queries.at[:, pl.ds(pl.multiple_of(role * 64, 64), 64), :], qv)
    load_c = load(cache, cv)
    load_g = [load(w_gate.at[pl.ds(i * SLICE, SLICE)], wg.at[pl.ds(i * SLICE, SLICE)]) for i in range(4)]
    load_u = [load(w_up.at[pl.ds(i * SLICE, SLICE)], wu.at[pl.ds(i * SLICE, SLICE)]) for i in range(4)]
    load_d = [load(w_down.at[pl.ds(i * 128, 128)], wd.at[pl.ds(i * 128, 128)]) for i in range(4)]

    barrier = pltpu.get_barrier_semaphore()
    partners = [(role, near(axis, d)) for axis in "xyz" for d in (1, 2, 3)]
    partners += [(1 - role, near("z", d)) for d in (0, 1, 2, 3)]
    for partner in partners:
        pl.semaphore_signal(barrier, inc=1, device_id=partner, device_id_type=MESH)

    hid = hidden[...].astype(F32)
    scale = lax.rsqrt(jnp.mean(jnp.square(hid), axis=-1, keepdims=True) + EPS)
    lane = lax.broadcasted_iota(jnp.int32, (8, 128), 1)
    table = jnp.zeros((8, 128), F32)
    for k in range(8):
        table = jnp.where(ids[:, k : k + 1] == lane % EXPERTS, gates[:, k : k + 1], table)
    extra = jnp.where(lane < 2 * EXPERTS, table, scale)
    own = jnp.where(role == 0, hid[0:4], hid[4:8])
    for i in range(4):
        xh[i] = own[:, i * SLICE : (i + 1) * SLICE].astype(BF16)
    xe[...] = jnp.where(role == 0, extra[0:4], extra[4:8])

    pl.semaphore_wait(barrier, len(partners))

    first = []
    for d in (2, 1, 3):
        first.append(go(remote(xh.at[plus("z", d)], yh.at[z], near("z", d))))
        first.append(go(remote(xe, ye.at[z], near("z", d))))

    def latent_copies():
        out = []
        for r, rows, axes in ((0, pl.ds(0, LOW_ROWS), "xy"), (1, pl.ds(LOW_ROWS, 112 - LOW_ROWS), "yx")):
            a, b = axes
            base = count[0]
            one = [
                remote(
                    wl.at[y, x, rows],
                    wl.at[y, x, rows],
                    near(a, d),
                )
                for d in (2, 1, 3)
            ]

            def place(pos, half, a=a, rows=rows):
                full = pl.ds(0, 4) if half is None else pl.ds(2 * half, 2)
                return wl.at[pos, full, rows] if a == "x" else wl.at[full, pos, rows]

            two = [remote(place(at[b], None), place(at[b], None), near(b, d)) for d in (1, 3)]
            three = [
                remote(place(plus(b, -1), 0), place(plus(b, -1), 0), near(b, 1)),
                remote(place(plus(b, 1), 1), place(plus(b, 1), 1), near(b, 3)),
            ]
            share = remote(wl.at[:, :, rows], wl.at[:, :, rows], dev, 1 - role)
            out.append((r, one, two, three, share))
            if r == 0:
                count[0] = base
        return out

    latent_plan = latent_copies()

    def latent_step(action):
        for r, one, two, three, share in latent_plan:

            @pl.when(role == r)
            def _(one=one, two=two, three=three, share=share):
                action(one, two, three, share)

    for r, rows in ((0, pl.ds(0, LOW_ROWS)), (1, pl.ds(LOW_ROWS, 112 - LOW_ROWS))):

        @pl.when(role == r)
        def _(rows=rows):
            own_rows = pltpu.make_async_copy(w_latent.at[rows], wl.at[y, x, rows], load_sems.at[15])
            own_rows.start()
            own_rows.wait()

    latent_step(lambda one, two, three, share: [c.start() for c in one])

    for copy in first:
        copy.wait_recv()
    yh[z] = xh[z]
    ye[z] = xe[...]
    h16 = jnp.concatenate([yh[i].astype(F32) for i in range(4)], axis=0)
    e16 = jnp.concatenate([ye[i] for i in range(4)], axis=0)
    hid16[...] = h16
    col = pl.ds(pl.multiple_of(z * SLICE, 128), SLICE)
    normed = (h16 * e16[:, 2 * EXPERTS : 2 * EXPERTS + 1] * ffn_gain[:, col]).astype(BF16)
    ga[z, x, y] = normed[:, 0:640]
    gb[z, x, y] = normed[:, 640:1280]
    gc[z, x, y, :, 0:512] = normed[:, 1280:1792]
    lane16 = lax.broadcasted_iota(jnp.int32, (16, 128), 1)
    high = e16.astype(BF16).astype(F32)
    gc[z, x, y, :, 512:640] = jnp.where(lane16 < EXPERTS, high, e16 - high).astype(BF16)

    gathered = (ga, gb, gc)

    def spot(order, k, value, half=None):
        spec = {}
        for axis in order[:k]:
            spec[axis] = pl.ds(0, 4)
        if half is not None:
            spec[order[0]] = pl.ds(2 * half, 2)
        spec[order[k]] = value
        for axis in order[k + 1 :]:
            spec[axis] = at[axis]
        return spec["z"], spec["x"], spec["y"]

    gstate = [None] * 3

    def gather_start(p, k):
        order, ref = GATHER[p], gathered[p]
        a = order[k]
        here = ref.at[spot(order, k, at[a])]
        copies = [go(remote(here, here, near(a, d))) for d in ((1, 3) if k else (2, 1, 3))]
        gstate[p] = copies

    def gather_forward(p, k):
        order, ref = GATHER[p], gathered[p]
        a = order[k]
        right, left = gstate[p]
        right.wait_recv()
        one = ref.at[spot(order, k, plus(a, -1), 0)]
        one = go(remote(one, one, near(a, 1)))
        left.wait_recv()
        two = ref.at[spot(order, k, plus(a, 1), 1)]
        two = go(remote(two, two, near(a, 3)))
        gstate[p] = [one, two]

    def gather_finish(p):
        for copy in gstate[p]:
            copy.wait_recv()

    def attend(lo, hi):
        @pl.loop(lo, hi)
        def _(i):
            s = lax.dot_general(qv[i], cv[i], (((1,), (1,)), ((), ())), preferred_element_type=F32)
            s = s * SCORE_SCALE
            live = lax.broadcasted_iota(jnp.int32, (64, 256), 1) < lengths[i]
            s = jnp.where(live, s, -jnp.inf)
            peak = jnp.max(s, axis=1, keepdims=True)
            w = jnp.where(live, jnp.exp(s - peak), 0.0).astype(BF16)
            sums[i] = jnp.broadcast_to(jnp.sum(w.astype(F32), axis=1, keepdims=True), (64, 128))
            peaks[i] = jnp.broadcast_to(peak, (64, 128))
            summed[i] = jnp.dot(w, cv[i, :, 0:LAT], preferred_element_type=F32)

    def gate_up(p, zz):
        rows = gathered[p][zz].reshape(256, 640)
        if p == 2:
            rows = rows[:, 0:512]
        k = pl.ds(pl.multiple_of(zz * SLICE + OFF[p], 128), WIDTH[p])
        acc_g[...] += jnp.dot(rows, wg[k, :], preferred_element_type=F32)
        acc_u[...] += jnp.dot(rows, wu[k, :], preferred_element_type=F32)

    for p in range(3):
        gather_start(p, 0)
    load_q.wait()
    load_c.wait()
    for p in range(3):
        gather_finish(p)
        gather_start(p, 1)
    attend(0, 4)
    for p in range(3):
        gather_forward(p, 1)
    attend(4, 8)
    for p in range(3):
        gather_finish(p)
        gather_start(p, 2)
    latent_step(lambda one, two, three, share: [c.wait_recv() for c in one])
    for copy in load_g + load_u:
        copy.wait()
    acc_g[...] = jnp.zeros_like(acc_g)
    acc_u[...] = jnp.zeros_like(acc_u)
    gate_up(0, z)
    for p in range(3):
        gather_forward(p, 2)
    latent_step(lambda one, two, three, share: [c.start() for c in two])
    gate_up(0, plus("z", 1))
    gate_up(0, plus("z", 3))
    for p in range(3):
        gather_finish(p)
    gate_up(0, plus("z", 2))
    for p in (1, 2):

        @pl.loop(0, 4)
        def _(zz, p=p):
            gate_up(p, zz)

    expert = z * 4 + y
    mine = lax.broadcasted_iota(jnp.int32, (256, 128), 1)
    mine = jnp.logical_or(mine == expert, mine == expert + EXPERTS)
    table_all = gc[0, :, :, :, 512:640].reshape(256, 128).astype(F32)
    gate_col[...] = jnp.sum(jnp.where(mine, table_all, 0.0), axis=1, keepdims=True)

    @pl.loop(0, 16)
    def _(i):
        rows = pl.ds(pl.multiple_of(i * 16, 16), 16)
        g = acc_g[rows, :]
        act[rows, :] = (g / (1.0 + jnp.exp(-g)) * acc_u[rows, :] * gate_col[rows, :]).astype(BF16)

    for copy in load_d:
        copy.wait()
    latent_step(
        lambda one, two, three, share: [
            two[0].wait_recv(),
            three[0].start(),
            two[1].wait_recv(),
            three[1].start(),
        ]
    )

    outs = (oa, ob, oc)

    def down(p, zz):
        k = pl.ds(pl.multiple_of(zz * SLICE + OFF[p], 128), WIDTH[p])
        out = jnp.dot(act[...], wd[:, k], preferred_element_type=F32)
        outs[p][zz] = out.astype(BF16).reshape(4, 4, 16, WIDTH[p])

    def block(order, s, value, half=None):
        spec = {}
        for axis in order[:s]:
            spec[axis] = pl.ds(0, 1)
        spec[order[s]] = pl.ds(value, 1)
        for axis in order[s + 1 :]:
            spec[axis] = pl.ds(0, 4)
        if half is not None:
            spec[order[2]] = pl.ds(2 * half, 2)
        return spec["z"], spec["x"], spec["y"]

    def part_of(order, half):
        spec = {axis: slice(None) for axis in order}
        spec[order[2]] = pl.ds(2 * half, 2)
        return spec["z"], spec["x"], spec["y"]

    sstate = [None] * 3

    def scatter_opposite(p, s, cur):
        order = SCATTER[p]
        b = order[s]
        fl, fr, rl, rr, out = rs_bufs[p][s]
        one = go(remote(cur.at[block(order, s, plus(b, 2), 0)], fl, near(b, 1)))
        two = go(remote(cur.at[block(order, s, plus(b, 2), 1)], fr, near(b, 3)))
        sstate[p] = [one, two]

    def scatter_direct(p, s, cur):
        order = SCATTER[p]
        b = order[s]
        fl, fr, rl, rr, out = rs_bufs[p][s]
        one = go(remote(cur.at[block(order, s, plus(b, 1), 1)], rl.at[part_of(order, 1)], near(b, 1)))
        two = go(remote(cur.at[block(order, s, plus(b, 3), 0)], rr.at[part_of(order, 0)], near(b, 3)))
        sstate[p] += [one, two]

    def add_into(dst, pieces):
        total = pieces[0].astype(F32)
        for piece in pieces[1:]:
            total = total + piece.astype(F32)
        dst[...] = total.astype(BF16)

    def scatter_forward(p, s, cur):
        order = SCATTER[p]
        b = order[s]
        fl, fr, rl, rr, out = rs_bufs[p][s]
        one, two, three, four = sstate[p]
        one.wait_recv()
        add_into(fl, [fl[...], cur[block(order, s, plus(b, 1), 0)]])
        one = go(remote(fl, rl.at[part_of(order, 0)], near(b, 1)))
        two.wait_recv()
        add_into(fr, [fr[...], cur[block(order, s, plus(b, 3), 1)]])
        two = go(remote(fr, rr.at[part_of(order, 1)], near(b, 3)))
        sstate[p] = [three, four, one, two]

    def scatter_finish(p, s, cur):
        order = SCATTER[p]
        b = order[s]
        fl, fr, rl, rr, out = rs_bufs[p][s]
        for copy in sstate[p]:
            copy.wait_recv()
        add_into(out, [cur[block(order, s, at[b])], rl[...], rr[...]])
        return out

    down(0, plus("z", 2))
    scatter_opposite(0, 0, oa)
    down(0, plus("z", 1))
    down(0, plus("z", 3))
    scatter_direct(0, 0, oa)
    for p in (1, 2):

        @pl.loop(0, 4)
        def _(zz, p=p):
            down(p, zz)

        scatter_opposite(p, 0, outs[p])
        scatter_direct(p, 0, outs[p])
    down(0, z)
    cur = list(outs)
    for p in range(3):
        scatter_forward(p, 0, cur[p])
    latent_step(lambda one, two, three, share: [three[0].wait_recv(), three[1].wait_recv(), share.start()])
    for s in (0, 1):
        for p in range(3):
            cur[p] = scatter_finish(p, s, cur[p])
            if s == 0:
                scatter_opposite(p, 1, cur[p])
                scatter_direct(p, 1, cur[p])
            else:
                order = SCATTER[p]
                b = order[2]
                slots = rs_bufs[p][2]
                sstate[p] = [
                    go(remote(cur[p].at[block(order, 2, plus(b, d))], slots.at[d - 1], near(b, d))) for d in (2, 1, 3)
                ]
        if s == 0:
            for p in range(3):
                scatter_forward(p, 1, cur[p])

    squares = jnp.zeros((16, 1), F32)
    for p in range(3):
        order = SCATTER[p]
        for copy in sstate[p]:
            copy.wait_recv()
        total = cur[p][block(order, 2, at[order[2]])].reshape(16, WIDTH[p]).astype(F32)
        for d in range(3):
            total = total + rs_bufs[p][2][d].reshape(16, WIDTH[p]).astype(F32)
        cols = slice(OFF[p], OFF[p] + WIDTH[p])
        residual = (hid16[:, cols] + total).astype(BF16).astype(F32)
        squares = squares + jnp.sum(jnp.square(residual), axis=1, keepdims=True)
        gain = attn_gain[:, pl.ds(pl.multiple_of(z * SLICE + OFF[p], 128), WIDTH[p])]
        att[:, cols] = (residual * gain).astype(BF16)
    for r, one, two, three, share in latent_plan:

        @pl.when(role == r)
        def _(r=r):
            rows = pl.ds(LOW_ROWS, 112 - LOW_ROWS) if r == 0 else pl.ds(0, LOW_ROWS)
            pltpu.make_async_remote_copy(
                src_ref=wl.at[:, :, rows],
                dst_ref=wl.at[:, :, rows],
                send_sem=send_sems.at[share_at],
                recv_sem=recv_sems.at[share_at],
                device_id=(1 - role, dev),
                device_id_type=MESH,
            ).wait_recv()

    partial = jnp.dot(att[...], wl[...].reshape(SLICE, KVW), preferred_element_type=F32)
    partial = jnp.concatenate([partial, jnp.broadcast_to(squares, (16, 64))], axis=1)
    for i in range(4):
        tbuf[i] = partial[4 * i : 4 * i + 4]

    last = []
    for d in (2, 1, 3, 0):
        for other in (0, 1):
            if d == 0 and other == 0:
                continue
            to_role = 1 - role if other else role
            last.append(go(remote(tbuf.at[plus("z", d)], ebuf.at[z, role], near("z", d), to_role)))
    ebuf[z, role] = tbuf[z]
    for copy in last:
        copy.wait_recv()
    halves = []
    for r in range(2):
        total = ebuf[0, r]
        for i in range(1, 4):
            total = total + ebuf[i, r]
        halves.append(total)
    comp = jnp.concatenate(halves, axis=0)
    comp = comp[:, 0:KVW] * lax.rsqrt(comp[:, KVW : KVW + 1] / D + EPS)
    content = comp[:, 0:LAT]
    content = content * lax.rsqrt(jnp.mean(jnp.square(content), axis=-1, keepdims=True) + EPS) * kv_gain[...]
    new_latent[:, 0:LAT] = content.astype(BF16)
    new_latent[:, LAT:KVW] = comp[:, LAT:KVW].astype(BF16)

    for i in range(8):
        row = new_latent[i : i + 1, :].astype(F32)
        score = jnp.sum(qv[i].astype(F32) * row, axis=1, keepdims=True) * SCORE_SCALE
        peak_cache = peaks[i][:, 0:1]
        peak = jnp.maximum(peak_cache, score)
        a = jnp.exp(peak_cache - peak)
        b = jnp.exp(score - peak)
        inv = 1.0 / (a * sums[i][:, 0:1] + b)
        context[i] = ((a * inv) * summed[i] + (b * inv) * row[:, 0:LAT]).astype(BF16)

    for copy in sent:
        copy.wait_send()
    latent_step(lambda one, two, three, share: [c.wait_send() for c in one + two + three + [share]])


share_at = 13


def shards(
    hidden_in,
    expert_ids,
    gate_values,
    ffn_gain,
    w_gate,
    w_up,
    w_down,
    attn_gain,
    w_latent,
    kv_gain,
    queries,
    cache,
    lengths,
):
    vmem = pl.BlockSpec(memory_space=pltpu.VMEM)
    smem = pl.BlockSpec(memory_space=pltpu.SMEM)
    hbm = pl.BlockSpec(memory_space=pl.ANY)
    v = pltpu.VMEM
    scatter_bufs = []
    for p in range(3):
        order, w = SCATTER[p], WIDTH[p]
        stages = []
        shape = [4, 4, 4]
        for s in (0, 1):
            shape[DIM[order[s]]] = 1
            half = list(shape)
            half[DIM[order[2]]] = 2
            full, half = (*shape, 16, w), (*half, 16, w)
            stages.append((v(half, BF16), v(half, BF16), v(full, BF16), v(full, BF16), v(full, BF16)))
        stages.append(v((3, 1, 1, 1, 16, w), BF16))
        scatter_bufs.append(tuple(stages))
    scratch = [
        v((D, FFD), BF16),
        v((D, FFD), BF16),
        v((FFD, D), BF16),
        v((4, 4, 112, KVW), BF16),
        v((8, 64, KVW), BF16),
        v((8, 256, KVW), BF16),
        v((8, 64, LAT), F32),
        v((8, 64, 128), F32),
        v((8, 64, 128), F32),
        v((4, 4, SLICE), BF16),
        v((4, 128), F32),
        v((4, 4, SLICE), BF16),
        v((4, 4, 128), F32),
        v((16, SLICE), F32),
        v((4, 4, 4, 16, 640), BF16),
        v((4, 4, 4, 16, 640), BF16),
        v((4, 4, 4, 16, 640), BF16),
        v((256, FFD), F32),
        v((256, FFD), F32),
        v((256, 1), F32),
        v((256, FFD), BF16),
        v((4, 4, 4, 16, WIDTH[0]), BF16),
        v((4, 4, 4, 16, WIDTH[1]), BF16),
        v((4, 4, 4, 16, WIDTH[2]), BF16),
        tuple(scatter_bufs),
        v((16, SLICE), BF16),
        v((4, 4, KVW + 64), F32),
        v((4, 2, 4, KVW + 64), F32),
        pltpu.SemaphoreType.DMA((128,)),
        pltpu.SemaphoreType.DMA((128,)),
        pltpu.SemaphoreType.DMA((16,)),
    ]
    return pl.pallas_call(
        kernel,
        out_shape=(
            jax.ShapeDtypeStruct((8, KVW), BF16),
            jax.ShapeDtypeStruct((8, 64, LAT), BF16),
        ),
        in_specs=[vmem] * 6 + [smem] + [hbm] * 6,
        out_specs=(vmem, vmem),
        scratch_shapes=scratch,
        compiler_params=pltpu.CompilerParams(
            collective_id=0,
            has_side_effects=True,
            vmem_limit_bytes=60 * 1024 * 1024,
        ),
        cost_estimate=pl.CostEstimate(flops=6 * 10**9, bytes_accessed=26 * 10**6, transcendentals=10**6),
    )(
        hidden_in,
        expert_ids,
        gate_values,
        ffn_gain.reshape(1, D),
        attn_gain.reshape(1, D),
        kv_gain.reshape(1, LAT),
        lengths,
        w_gate,
        w_up,
        w_down,
        w_latent,
        queries,
        cache,
    )


def solution(mesh):
    in_specs = (
        P("dev", None),
        P("dev", None),
        P("dev", None),
        P(),
        P(None, "dev"),
        P(None, "dev"),
        P("dev", None),
        P(),
        P("dev", None),
        P(),
        P("dev", None, None),
        P("dev", None, None),
        P("dev"),
    )
    out_specs = (P("dev", None), P("dev", "role", None))
    return jax.shard_map(shards, mesh=mesh, in_specs=in_specs, out_specs=out_specs, check_vma=False)
```

```python
import jax
import jax.numpy as jnp
from jax import lax
from jax.experimental import pallas as pl
from jax.experimental.pallas import tpu as pltpu
from jax.sharding import PartitionSpec as P

MESH = pl.DeviceIdType.MESH
F32 = jnp.float32
BF16 = jnp.bfloat16

SCORE_SCALE = 192.0 ** (-0.5)
EPS = 1e-06
D = 7168
SLICE = 1792
FFD = 512
LAT = 512
KVW = 576
EXPERTS = 16
WIDTH = (640, 640, 512)
OFF = (0, 640, 1280)
BASE = (0, 2560, 5120)
GATHER = (("x", "y", "z"), ("y", "z", "x"), ("z", "x", "y"))
SCATTER = tuple(order[::-1] for order in GATHER)
HALVED = ("x", "z", "z")
DIM = {"z": 0, "x": 1, "y": 2}
LOW_ROWS = 64


def kernel(
    hidden,
    ids,
    gates,
    ffn_gain,
    attn_gain,
    kv_gain,
    lengths,
    w_gate,
    w_up,
    w_down,
    w_latent,
    queries,
    cache,
    new_latent,
    context,
    wgu,
    wd,
    wl,
    qt,
    qv,
    cv,
    summed,
    peaks,
    sums,
    xh,
    xe,
    yh,
    ye,
    hid16,
    ga,
    gb,
    gc,
    acc,
    gate_col,
    act,
    oa,
    ob,
    oc,
    rs_bufs,
    att,
    tbuf,
    ebuf,
    send_sems,
    recv_sems,
    load_sems,
):
    role = lax.axis_index("role")
    dev = lax.axis_index("dev")
    z, y, x = dev // 16, lax.rem(dev // 4, 4), lax.rem(dev, 4)
    at = {"z": z, "y": y, "x": x}
    stride = {"z": 16, "y": 4, "x": 1}

    def plus(axis, d):
        return lax.rem(at[axis] + (d + 4), 4)

    def near(axis, d):
        return dev + (plus(axis, d) - at[axis]) * stride[axis]

    count = [0]
    sent = []

    def remote(src, dst, to_dev, to_role=None):
        i = count[0]
        count[0] += 1
        return pltpu.make_async_remote_copy(
            src_ref=src,
            dst_ref=dst,
            send_sem=send_sems.at[i],
            recv_sem=recv_sems.at[i],
            device_id=(role if to_role is None else to_role, to_dev),
            device_id_type=MESH,
        )

    def go(copy):
        copy.start()
        sent.append(copy)
        return copy

    loads = []

    def load(src, dst):
        copy = pltpu.make_async_copy(src, dst, load_sems.at[len(loads)])
        copy.start(priority=1)
        loads.append(copy)
        return copy

    load_q = load(queries, qt)
    load_c = load(cache, cv)
    barrier = pltpu.get_barrier_semaphore()
    partners = [(role, near(axis, d)) for axis in "xyz" for d in (1, 2, 3)]
    partners += [(1 - role, near("z", d)) for d in (0, 1, 2, 3)]
    for partner in partners:
        pl.semaphore_signal(barrier, inc=1, device_id=partner, device_id_type=MESH)

    hid = hidden[...].astype(F32)
    scale = lax.rsqrt(jnp.mean(jnp.square(hid), axis=-1, keepdims=True) + EPS)
    lane = lax.broadcasted_iota(jnp.int32, (8, 128), 1)
    table = jnp.zeros((8, 128), F32)
    for k in range(8):
        table = jnp.where(ids[:, k : k + 1] == lane % EXPERTS, gates[:, k : k + 1], table)
    extra = jnp.where(lane < 2 * EXPERTS, table, scale)
    own = jnp.where(role == 0, hid[0:4], hid[4:8])
    for i in range(4):
        xh[i] = own[:, i * SLICE : (i + 1) * SLICE].astype(BF16)
    xe[...] = jnp.where(role == 0, extra[0:4], extra[4:8])

    pl.semaphore_wait(barrier, len(partners))

    first = []
    for d in (2, 1, 3):
        first.append(go(remote(xh.at[plus("z", d)], yh.at[z], near("z", d))))
        first.append(go(remote(xe, ye.at[z], near("z", d))))

    load_gu, load_d = [], []
    pieces = [(p, i) for p in range(3) for i in range(4)]
    for p, i in pieces:
        here, there = pl.ds(i * SLICE + OFF[p], WIDTH[p]), pl.ds(BASE[p] + i * WIDTH[p], WIDTH[p])
        load_gu.append(load(w_gate.at[here], wgu.at[there, pl.ds(0, FFD)]))
        load_gu.append(load(w_up.at[here], wgu.at[there, pl.ds(FFD, FFD)]))
    for p, i in pieces:
        here, there = pl.ds(i * SLICE + OFF[p], WIDTH[p]), pl.ds(BASE[p] + i * WIDTH[p], WIDTH[p])
        load_d.append(load(w_down.at[:, here], wd.at[:, there]))

    def latent_copies():
        out = []
        for r, rows, axes in ((0, pl.ds(0, LOW_ROWS), "xy"), (1, pl.ds(LOW_ROWS, 112 - LOW_ROWS), "yx")):
            a, b = axes
            base = count[0]
            one = [
                remote(
                    wl.at[y, x, rows],
                    wl.at[y, x, rows],
                    near(a, d),
                )
                for d in (2, 1, 3)
            ]

            def place(pos, half, a=a, rows=rows):
                full = pl.ds(2 * half, 2)
                return wl.at[pos, full, rows] if a == "x" else wl.at[full, pos, rows]

            def send(pos, half, d, b=b, place=place):
                return remote(place(pos, half), place(pos, half), near(b, d))

            two = [send(at[b], 0, 1), send(at[b], 1, 3), send(at[b], 1, 1), send(at[b], 0, 3)]
            three = [send(plus(b, -1), 0, 1), send(plus(b, 1), 1, 3)]
            share = remote(wl.at[:, :, rows], wl.at[:, :, rows], dev, 1 - role)
            out.append((r, one, two, three, share))
            if r == 0:
                count[0] = base
        return out

    latent_plan = latent_copies()

    def latent_step(action):
        for r, one, two, three, share in latent_plan:

            @pl.when(role == r)
            def _(one=one, two=two, three=three, share=share):
                action(one, two, three, share)

    for r, rows in ((0, pl.ds(0, LOW_ROWS)), (1, pl.ds(LOW_ROWS, 112 - LOW_ROWS))):

        @pl.when(role == r)
        def _(rows=rows):
            own_rows = pltpu.make_async_copy(w_latent.at[rows], wl.at[y, x, rows], load_sems.at[63])
            own_rows.start()
            own_rows.wait()

    latent_step(lambda one, two, three, share: [c.start() for c in one])

    for copy in first:
        copy.wait_recv()
    yh[z] = xh[z]
    ye[z] = xe[...]
    h16 = jnp.concatenate([yh[i].astype(F32) for i in range(4)], axis=0)
    e16 = jnp.concatenate([ye[i] for i in range(4)], axis=0)
    hid16[...] = h16
    col = pl.ds(pl.multiple_of(z * SLICE, 128), SLICE)
    normed = (h16 * e16[:, 2 * EXPERTS : 2 * EXPERTS + 1] * ffn_gain[:, col]).astype(BF16)
    ga[z, x, y] = normed[:, 0:640]
    gb[z, x, y] = normed[:, 640:1280]
    gc[z, x, y, :, 0:512] = normed[:, 1280:1792]
    lane16 = lax.broadcasted_iota(jnp.int32, (16, 128), 1)
    high = e16.astype(BF16).astype(F32)
    gc[z, x, y, :, 512:640] = jnp.where(lane16 < EXPERTS, high, e16 - high).astype(BF16)

    gathered = (ga, gb, gc)

    def spot(order, k, value, half=None):
        spec = {}
        for axis in order[:k]:
            spec[axis] = pl.ds(0, 4)
        if half is not None:
            spec[order[0]] = pl.ds(2 * half, 2)
        spec[order[k]] = value
        for axis in order[k + 1 :]:
            spec[axis] = at[axis]
        return spec["z"], spec["x"], spec["y"]

    gstate = [None] * 3

    def gather_start(p, k):
        order, ref = GATHER[p], gathered[p]
        a = order[k]
        if k < 2:
            here = ref.at[spot(order, k, at[a])]
            gstate[p] = [go(remote(here, here, near(a, d))) for d in (2, 1, 3)]
            return
        gstate[p] = []
        for half, d in ((0, 1), (1, 3)):
            here = ref.at[spot(order, k, at[a], half)]
            gstate[p].append(go(remote(here, here, near(a, d))))

    def gather_rest(p, k):
        order, ref = GATHER[p], gathered[p]
        a = order[k]
        for half, d in ((1, 1), (0, 3)):
            here = ref.at[spot(order, k, at[a], half)]
            gstate[p].append(go(remote(here, here, near(a, d))))

    def gather_forward(p, k):
        order, ref = GATHER[p], gathered[p]
        a = order[k]
        gstate[p][0].wait_recv()
        one = ref.at[spot(order, k, plus(a, -1), 0)]
        one = go(remote(one, one, near(a, 1)))
        gstate[p][1].wait_recv()
        two = ref.at[spot(order, k, plus(a, 1), 1)]
        two = go(remote(two, two, near(a, 3)))
        gstate[p] = gstate[p][2:] + [one, two]

    def gather_wait(p, n):
        for copy in gstate[p][:n]:
            copy.wait_recv()
        gstate[p] = gstate[p][n:]

    def attend(lo, hi):
        @pl.loop(lo, hi)
        def _(i):
            both = qt[i].T
            qv[i] = jnp.where(role == 0, both[0:64], both[64:128])
            s = jnp.dot(qv[i], cv[i], preferred_element_type=F32)
            s = s * SCORE_SCALE
            live = lax.broadcasted_iota(jnp.int32, (64, 256), 1) < lengths[i]
            s = jnp.where(live, s, -jnp.inf)
            peak = jnp.max(s, axis=1, keepdims=True)
            w = jnp.where(live, jnp.exp(s - peak), 0.0).astype(BF16)
            sums[i] = jnp.broadcast_to(jnp.sum(w.astype(F32), axis=1, keepdims=True), (64, 128))
            peaks[i] = jnp.broadcast_to(peak, (64, 128))
            summed[i] = lax.dot_general(
                w, cv[i, 0:LAT, :], (((1,), (1,)), ((), ())), preferred_element_type=F32
            )

    def gate_up_slice(zz, first=False):
        k = pl.ds(pl.multiple_of(BASE[0] + zz * WIDTH[0], 128), WIDTH[0])

        @pl.loop(0, 2)
        def _(n):
            cols = pl.ds(pl.multiple_of(n * 512, 512), 512)
            rows = ga[zz].reshape(256, WIDTH[0])
            out = jnp.dot(rows, wgu[k, cols], preferred_element_type=F32).reshape(4, 4, 16, 512)
            acc[..., cols] = out if first else acc[..., cols] + out

    def gate_up_rows(*ds):
        for p in (1, 2):
            picks = []
            for d in ds:
                axis = GATHER[p][2]
                picks.append((plus("x", d), slice(None)) if axis == "x" else (slice(None), plus("y", d)))

            @pl.loop(0, 1)
            def _(n, p=p, picks=picks):
                cols = pl.ds(pl.multiple_of(n * 1024, 1024), 1024)
                rows = [
                    jnp.concatenate(
                        [gathered[p][i, a, b, :, 0 : WIDTH[p]].reshape(64, WIDTH[p]) for i in range(4)], axis=1
                    )
                    for a, b in picks
                ]
                rows = jnp.concatenate(rows, axis=0) if len(rows) > 1 else rows[0]
                out = jnp.dot(rows, wgu[pl.ds(BASE[p], 4 * WIDTH[p]), cols], preferred_element_type=F32)
                for i, (a, b) in enumerate(picks):
                    acc[a, b, :, cols] += out[64 * i : 64 * i + 64].reshape(4, 16, 1024)

    for p in range(3):
        gather_start(p, 0)
    load_q.wait()
    load_c.wait()
    attend(0, 4)
    for p in range(3):
        gather_wait(p, 3)
        gather_start(p, 1)
    latent_step(lambda one, two, three, share: [c.wait_recv() for c in one] + [c.start() for c in two])
    attend(4, 8)
    for p in range(3):
        gather_wait(p, 3)
        gather_start(p, 2)
    for p in range(3):
        gather_rest(p, 2)
    for copy in load_gu:
        copy.wait()
    gate_up_slice(z, True)
    gate_up_rows(0)
    for p in range(3):
        gather_forward(p, 2)
    latent_step(
        lambda one, two, three, share: [
            two[0].wait_recv(),
            three[0].start(),
            two[1].wait_recv(),
            three[1].start(),
        ]
    )
    for p in range(3):
        gather_wait(p, 2)
    gate_up_slice(plus("z", 1))
    gate_up_slice(plus("z", 3))
    gate_up_rows(1, 3)
    gather_wait(0, 2)
    gate_up_slice(plus("z", 2))
    gather_wait(1, 2)
    gather_wait(2, 2)
    gate_up_rows(2)

    expert = z * 4 + y
    mine = lax.broadcasted_iota(jnp.int32, (256, 128), 1)
    mine = jnp.logical_or(mine == expert, mine == expert + EXPERTS)
    table_all = gc[0, :, :, :, 512:640].reshape(256, 128).astype(F32)
    gate_col[...] = jnp.sum(jnp.where(mine, table_all, 0.0), axis=1, keepdims=True)

    @pl.loop(0, 8)
    def _(i):
        rows = pl.ds(pl.multiple_of(i * 32, 32), 32)
        half = pl.ds(pl.multiple_of(lax.rem(i, 2) * 2, 2), 2)
        g = acc[i // 2, half, :, 0:FFD].reshape(32, FFD)
        u = acc[i // 2, half, :, FFD:].reshape(32, FFD)
        act[rows, :] = (g / (1.0 + jnp.exp(-g)) * u * gate_col[rows, :]).astype(BF16)

    for copy in load_d:
        copy.wait()

    outs = (oa, ob, oc)

    def down(p, zz, n=1):
        k = pl.ds(pl.multiple_of(BASE[p] + zz * WIDTH[p], 128), n * WIDTH[p])
        out = jnp.dot(act[...], wd[:, k], preferred_element_type=F32).astype(BF16)
        for i in range(n):
            outs[p][zz + i] = out[:, i * WIDTH[p] : (i + 1) * WIDTH[p]].reshape(4, 4, 16, WIDTH[p])

    def block(order, s, value, half=None):
        spec = {}
        for axis in order[:s]:
            spec[axis] = pl.ds(0, 1)
        spec[order[s]] = pl.ds(value, 1)
        for axis in order[s + 1 :]:
            spec[axis] = pl.ds(0, 4)
        if half is not None:
            spec[HALVED[SCATTER.index(order)]] = pl.ds(2 * half, 2)
        return spec["z"], spec["x"], spec["y"]

    def part_of(order, half):
        spec = {axis: slice(None) for axis in order}
        spec[HALVED[SCATTER.index(order)]] = pl.ds(2 * half, 2)
        return spec["z"], spec["x"], spec["y"]

    sstate = [[], [], []]

    def scatter_opposite(p, s, cur, half):
        order = SCATTER[p]
        b = order[s]
        to = rs_bufs[p][s][half]
        d = (1, 3)[half]
        sstate[p].append(go(remote(cur.at[block(order, s, plus(b, 2), half)], to, near(b, d))))

    def scatter_direct(p, s, cur):
        order = SCATTER[p]
        b = order[s]
        fl, fr, rl, rr, out = rs_bufs[p][s]
        one = go(remote(cur.at[block(order, s, plus(b, 1), 1)], rl.at[part_of(order, 1)], near(b, 1)))
        two = go(remote(cur.at[block(order, s, plus(b, 3), 0)], rr.at[part_of(order, 0)], near(b, 3)))
        sstate[p] += [one, two]

    def add_into(dst, pieces):
        total = pieces[0].astype(F32)
        for piece in pieces[1:]:
            total = total + piece.astype(F32)
        dst[...] = total.astype(BF16)

    def scatter_forward(p, s, cur):
        order = SCATTER[p]
        b = order[s]
        fl, fr, rl, rr, out = rs_bufs[p][s]
        one, two, three, four = sstate[p]
        one.wait_recv()
        add_into(fl, [fl[...], cur[block(order, s, plus(b, 1), 0)]])
        one = go(remote(fl, rl.at[part_of(order, 0)], near(b, 1)))
        two.wait_recv()
        add_into(fr, [fr[...], cur[block(order, s, plus(b, 3), 1)]])
        two = go(remote(fr, rr.at[part_of(order, 1)], near(b, 3)))
        sstate[p] = [three, four, one, two]

    def scatter_finish(p, s, cur):
        order = SCATTER[p]
        b = order[s]
        fl, fr, rl, rr, out = rs_bufs[p][s]
        for copy in sstate[p]:
            copy.wait_recv()
        add_into(out, [cur[block(order, s, at[b])], rl[...], rr[...]])
        return out

    down(0, plus("z", 2))
    scatter_opposite(0, 0, oa, 0)
    scatter_opposite(0, 0, oa, 1)
    for p in (1, 2):
        for half in (0, 1):
            down(p, 2 * half, 2)
            scatter_opposite(p, 0, outs[p], half)
        scatter_direct(p, 0, outs[p])
    down(0, plus("z", 1))
    down(0, plus("z", 3))
    scatter_direct(0, 0, oa)
    down(0, z)
    cur = list(outs)
    for p in range(3):
        scatter_forward(p, 0, cur[p])
    latent_step(lambda one, two, three, share: [c.wait_recv() for c in two[2:] + three] + [share.start()])
    def scatter_all(p, s):
        order = SCATTER[p]
        b = order[s]
        slots = rs_bufs[p][s][0]
        sstate[p] = [
            go(remote(cur[p].at[block(order, s, plus(b, d))], slots.at[d - 1], near(b, d))) for d in (2, 1, 3)
        ]

    for p in range(3):
        cur[p] = scatter_finish(p, 0, cur[p])
        scatter_all(p, 1)
    for p in range(3):
        order = SCATTER[p]
        slots, out = rs_bufs[p][1]
        for copy in sstate[p]:
            copy.wait_recv()
        add_into(out, [cur[p][block(order, 1, at[order[1]])]] + [slots[d] for d in range(3)])
        cur[p] = out
        scatter_all(p, 2)

    squares = jnp.zeros((16, 1), F32)
    for p in range(3):
        order = SCATTER[p]
        for copy in sstate[p]:
            copy.wait_recv()
        total = cur[p][block(order, 2, at[order[2]])].reshape(16, WIDTH[p]).astype(F32)
        for d in range(3):
            total = total + rs_bufs[p][2][0][d].reshape(16, WIDTH[p]).astype(F32)
        cols = slice(OFF[p], OFF[p] + WIDTH[p])
        residual = (hid16[:, cols] + total).astype(BF16).astype(F32)
        squares = squares + jnp.sum(jnp.square(residual), axis=1, keepdims=True)
        gain = attn_gain[:, pl.ds(pl.multiple_of(z * SLICE + OFF[p], 128), WIDTH[p])]
        att[:, cols] = (residual * gain).astype(BF16)
    for r, one, two, three, share in latent_plan:

        @pl.when(role == r)
        def _(r=r):
            rows = pl.ds(LOW_ROWS, 112 - LOW_ROWS) if r == 0 else pl.ds(0, LOW_ROWS)
            pltpu.make_async_remote_copy(
                src_ref=wl.at[:, :, rows],
                dst_ref=wl.at[:, :, rows],
                send_sem=send_sems.at[share_at],
                recv_sem=recv_sems.at[share_at],
                device_id=(1 - role, dev),
                device_id_type=MESH,
            ).wait_recv()

    partial = jnp.dot(att[...], wl[...].reshape(SLICE, KVW), preferred_element_type=F32)
    partial = jnp.concatenate([partial, jnp.broadcast_to(squares, (16, 64))], axis=1)
    for i in range(4):
        tbuf[i] = partial[4 * i : 4 * i + 4]

    last = []
    for d in (2, 1, 3, 0):
        for other in (0, 1):
            if d == 0 and other == 0:
                continue
            to_role = 1 - role if other else role
            last.append(go(remote(tbuf.at[plus("z", d)], ebuf.at[z, role], near("z", d), to_role)))
    ebuf[z, role] = tbuf[z]
    for copy in last:
        copy.wait_recv()
    halves = []
    for r in range(2):
        total = ebuf[0, r]
        for i in range(1, 4):
            total = total + ebuf[i, r]
        halves.append(total)
    comp = jnp.concatenate(halves, axis=0)
    comp = comp[:, 0:KVW] * lax.rsqrt(comp[:, KVW : KVW + 1] / D + EPS)
    content = comp[:, 0:LAT]
    content = content * lax.rsqrt(jnp.mean(jnp.square(content), axis=-1, keepdims=True) + EPS) * kv_gain[...]
    new_latent[:, 0:LAT] = content.astype(BF16)
    new_latent[:, LAT:KVW] = comp[:, LAT:KVW].astype(BF16)

    for i in range(8):
        row = new_latent[i : i + 1, :].astype(F32)
        score = jnp.sum(qv[i].astype(F32) * row, axis=1, keepdims=True) * SCORE_SCALE
        peak_cache = peaks[i][:, 0:1]
        peak = jnp.maximum(peak_cache, score)
        a = jnp.exp(peak_cache - peak)
        b = jnp.exp(score - peak)
        inv = 1.0 / (a * sums[i][:, 0:1] + b)
        context[i] = ((a * inv) * summed[i] + (b * inv) * row[:, 0:LAT]).astype(BF16)

    for copy in sent:
        copy.wait_send()
    latent_step(lambda one, two, three, share: [c.wait_send() for c in one + two + three + [share]])


share_at = 15


def shards(
    hidden_in,
    expert_ids,
    gate_values,
    ffn_gain,
    w_gate,
    w_up,
    w_down,
    attn_gain,
    w_latent,
    kv_gain,
    queries,
    cache,
    lengths,
):
    vmem = pl.BlockSpec(memory_space=pltpu.VMEM)
    smem = pl.BlockSpec(memory_space=pltpu.SMEM)
    hbm = pl.BlockSpec(memory_space=pl.ANY)
    v = pltpu.VMEM
    scatter_bufs = []
    for p in range(3):
        order, w = SCATTER[p], WIDTH[p]
        stages = []
        shape = [4, 4, 4]
        for s in range(3):
            shape[DIM[order[s]]] = 1
            full = (*shape, 16, w)
            half = list(full)
            half[DIM[HALVED[p]]] = 2
            if s == 0:
                stages.append((v(half, BF16), v(half, BF16), v(full, BF16), v(full, BF16), v(full, BF16)))
            elif s == 1:
                stages.append((v((3, *full), BF16), v(full, BF16)))
            else:
                stages.append((v((3, *full), BF16),))
        scatter_bufs.append(tuple(stages))
    scratch = [
        v((D, 2 * FFD), BF16),
        v((FFD, D), BF16),
        v((4, 4, 112, KVW), BF16),
        v((8, KVW, 128), BF16),
        v((8, 64, KVW), BF16),
        v((8, KVW, 256), BF16),
        v((8, 64, LAT), F32),
        v((8, 64, 128), F32),
        v((8, 64, 128), F32),
        v((4, 4, SLICE), BF16),
        v((4, 128), F32),
        v((4, 4, SLICE), BF16),
        v((4, 4, 128), F32),
        v((16, SLICE), F32),
        v((4, 4, 4, 16, 640), BF16),
        v((4, 4, 4, 16, 640), BF16),
        v((4, 4, 4, 16, 640), BF16),
        v((4, 4, 16, 2 * FFD), F32),
        v((256, 1), F32),
        v((256, FFD), BF16),
        v((4, 4, 4, 16, WIDTH[0]), BF16),
        v((4, 4, 4, 16, WIDTH[1]), BF16),
        v((4, 4, 4, 16, WIDTH[2]), BF16),
        tuple(scatter_bufs),
        v((16, SLICE), BF16),
        v((4, 4, KVW + 64), F32),
        v((4, 2, 4, KVW + 64), F32),
        pltpu.SemaphoreType.DMA((128,)),
        pltpu.SemaphoreType.DMA((128,)),
        pltpu.SemaphoreType.DMA((64,)),
    ]
    return pl.pallas_call(
        kernel,
        out_shape=(
            jax.ShapeDtypeStruct((8, KVW), BF16),
            jax.ShapeDtypeStruct((8, 64, LAT), BF16),
        ),
        in_specs=[vmem] * 6 + [smem] + [hbm] * 6,
        out_specs=(vmem, vmem),
        scratch_shapes=scratch,
        compiler_params=pltpu.CompilerParams(
            collective_id=0,
            has_side_effects=True,
            vmem_limit_bytes=60 * 1024 * 1024,
        ),
        cost_estimate=pl.CostEstimate(flops=6 * 10**9, bytes_accessed=26 * 10**6, transcendentals=10**6),
    )(
        hidden_in,
        expert_ids,
        gate_values,
        ffn_gain.reshape(1, D),
        attn_gain.reshape(1, D),
        kv_gain.reshape(1, LAT),
        lengths,
        w_gate,
        w_up,
        w_down,
        w_latent,
        jnp.transpose(queries, (0, 2, 1)),
        jnp.transpose(cache, (0, 2, 1)),
    )


def solution(mesh):
    in_specs = (
        P("dev", None),
        P("dev", None),
        P("dev", None),
        P(),
        P(None, "dev"),
        P(None, "dev"),
        P("dev", None),
        P(),
        P("dev", None),
        P(),
        P("dev", None, None),
        P("dev", None, None),
        P("dev"),
    )
    out_specs = (P("dev", None), P("dev", "role", None))
    return jax.shard_map(shards, mesh=mesh, in_specs=in_specs, out_specs=out_specs, check_vma=False)
```

```python
import jax
import jax.numpy as jnp
from jax import lax
from jax.experimental import pallas as pl
from jax.experimental.pallas import tpu as pltpu
from jax.sharding import PartitionSpec as P

MESH = pl.DeviceIdType.MESH
F32 = jnp.float32
BF16 = jnp.bfloat16

SCORE_SCALE = 192.0 ** (-0.5)
EPS = 1e-06
D = 7168
SLICE = 1792
FFD = 512
LAT = 512
KVW = 576
EXPERTS = 16
WIDTH = (640, 640, 512)
OFF = (0, 640, 1280)
BASE = (0, 2560, 5120)
GATHER = (("x", "y", "z"), ("y", "z", "x"), ("z", "x", "y"))
SCATTER = tuple(order[::-1] for order in GATHER)
HALVED = ("x", "z", "z")
DIM = {"z": 0, "x": 1, "y": 2}
SEND_RING = 44
COPIES = 95
LOADS = 46
LOW_ROWS = 64


def kernel(
    hidden_in,
    ids_in,
    gates_in,
    ffn_gain_in,
    attn_gain_in,
    kv_gain_in,
    lengths,
    w_gate,
    w_up,
    w_down,
    w_latent,
    queries,
    cache,
    new_latent,
    factors,
    summed_out,
    hidden,
    ids,
    gates,
    ffn_gain,
    attn_gain,
    kv_gain,
    wgu,
    wd,
    wl,
    qt,
    qv,
    cv,
    summed,
    peaks,
    sums,
    xh,
    xe,
    yh,
    ye,
    hid16,
    ga,
    gb,
    gc,
    acc,
    gate_col,
    act,
    oa,
    ob,
    oc,
    rs_bufs,
    tbuf,
    ebuf,
    send_sems,
    recv_sems,
    load_sems,
):
    role = lax.axis_index("role")
    dev = lax.axis_index("dev")
    z, y, x = dev // 16, lax.rem(dev // 4, 4), lax.rem(dev, 4)
    at = {"z": z, "y": y, "x": x}
    stride = {"z": 16, "y": 4, "x": 1}

    def plus(axis, d):
        return lax.rem(at[axis] + (d + 4), 4)

    def near(axis, d):
        return dev + (plus(axis, d) - at[axis]) * stride[axis]

    count = [0]
    sent = []

    def remote(src, dst, to_dev, to_role=None, send_at=None):
        i = count[0]
        count[0] += 1
        if send_at is None:
            if len(sent) >= SEND_RING:
                sent[-SEND_RING].wait_send()
            send_at = len(sent) % SEND_RING
        return pltpu.make_async_remote_copy(
            src_ref=src,
            dst_ref=dst,
            send_sem=send_sems.at[send_at],
            recv_sem=recv_sems.at[i],
            device_id=(role if to_role is None else to_role, to_dev),
            device_id_type=MESH,
        )

    def go(copy):
        copy.start()
        sent.append(copy)
        return copy

    loads = []

    def load(src, dst):
        copy = pltpu.make_async_copy(src, dst, load_sems.at[len(loads)])
        copy.start(priority=1)
        loads.append(copy)
        return copy

    barrier = pltpu.get_barrier_semaphore()
    partners = [(role, near(axis, d)) for axis in "xyz" for d in (1, 2, 3)]
    partners += [(1 - role, near("z", d)) for d in (0, 1, 2, 3)]
    for partner in partners:
        pl.semaphore_signal(barrier, inc=1, device_id=partner, device_id_type=MESH)

    small = (
        load(hidden_in, hidden),
        load(ids_in, ids),
        load(gates_in, gates),
        load(ffn_gain_in, ffn_gain),
        load(attn_gain_in, attn_gain),
        load(kv_gain_in, kv_gain),
    )
    load_q = load(queries, qt)
    load_c = load(cache, cv)

    for copy in small:
        copy.wait()
    hid = hidden[...].astype(F32)
    scale = lax.rsqrt(jnp.mean(jnp.square(hid), axis=-1, keepdims=True) + EPS)
    lane = lax.broadcasted_iota(jnp.int32, (8, 128), 1)
    table = jnp.zeros((8, 128), F32)
    for k in range(8):
        table = jnp.where(ids[:, k : k + 1] == lane % EXPERTS, gates[:, k : k + 1], table)
    extra = jnp.where(lane < 2 * EXPERTS, table, scale)
    own = jnp.where(role == 0, hid[0:4], hid[4:8])
    for i in range(4):
        xh[i] = own[:, i * SLICE : (i + 1) * SLICE].astype(BF16)
    xe[...] = jnp.where(role == 0, extra[0:4], extra[4:8])

    pl.semaphore_wait(barrier, len(partners))

    first = []
    for d in (2, 1, 3):
        first.append(go(remote(xh.at[plus("z", d)], yh.at[z], near("z", d))))
        first.append(go(remote(xe, ye.at[z], near("z", d))))

    load_gu, load_d = [], []
    pieces = [(p, i) for p in range(3) for i in range(4)]
    for p, i in pieces:
        here, there = pl.ds(i * SLICE + OFF[p], WIDTH[p]), pl.ds(BASE[p] + i * WIDTH[p], WIDTH[p])
        load_gu.append(load(w_gate.at[here], wgu.at[there, pl.ds(0, FFD)]))
        load_gu.append(load(w_up.at[here], wgu.at[there, pl.ds(FFD, FFD)]))
    for p, i in pieces:
        here, there = pl.ds(i * SLICE + OFF[p], WIDTH[p]), pl.ds(BASE[p] + i * WIDTH[p], WIDTH[p])
        load_d.append(load(w_down.at[:, here], wd.at[:, there]))

    def latent_copies():
        out = []
        for r, rows, axes in ((0, pl.ds(0, LOW_ROWS), "xy"), (1, pl.ds(LOW_ROWS, 112 - LOW_ROWS), "yx")):
            a, b = axes
            base = count[0]
            one = [
                remote(
                    wl.at[y, x, rows],
                    wl.at[y, x, rows],
                    near(a, d),
                    send_at=SEND_RING + d - 1,
                )
                for d in (2, 1, 3)
            ]

            def place(pos, half, a=a, rows=rows):
                full = pl.ds(2 * half, 2)
                return wl.at[pos, full, rows] if a == "x" else wl.at[full, pos, rows]

            def send(pos, half, d, k, b=b, place=place):
                return remote(place(pos, half), place(pos, half), near(b, d), send_at=SEND_RING + k)

            two = [send(at[b], 0, 1, 3), send(at[b], 1, 3, 4), send(at[b], 1, 1, 5), send(at[b], 0, 3, 6)]
            three = [send(plus(b, -1), 0, 1, 7), send(plus(b, 1), 1, 3, 8)]
            share = remote(wl.at[:, :, rows], wl.at[:, :, rows], dev, 1 - role, SEND_RING + 9)
            out.append((r, one, two, three, share))
            if r == 0:
                count[0] = base
        return out

    latent_plan = latent_copies()

    def latent_step(action):
        for r, one, two, three, share in latent_plan:

            @pl.when(role == r)
            def _(one=one, two=two, three=three, share=share):
                action(one, two, three, share)

    for r, rows in ((0, pl.ds(0, LOW_ROWS)), (1, pl.ds(LOW_ROWS, 112 - LOW_ROWS))):

        @pl.when(role == r)
        def _(rows=rows):
            own_rows = pltpu.make_async_copy(w_latent.at[rows], wl.at[y, x, rows], load_sems.at[LOADS - 1])
            own_rows.start()
            own_rows.wait()

    latent_step(lambda one, two, three, share: [c.start() for c in one])

    for copy in first:
        copy.wait_recv()
    yh[z] = xh[z]
    ye[z] = xe[...]
    h16 = jnp.concatenate([yh[i].astype(F32) for i in range(4)], axis=0)
    e16 = jnp.concatenate([ye[i] for i in range(4)], axis=0)
    hid16[...] = h16
    col = pl.ds(pl.multiple_of(z * SLICE, 128), SLICE)
    normed = (h16 * e16[:, 2 * EXPERTS : 2 * EXPERTS + 1] * ffn_gain[:, col]).astype(BF16)
    ga[z, x, y] = normed[:, 0:640]
    gb[z, x, y] = normed[:, 640:1280]
    gc[z, x, y, :, 0:512] = normed[:, 1280:1792]
    lane16 = lax.broadcasted_iota(jnp.int32, (16, 128), 1)
    high = e16.astype(BF16).astype(F32)
    gc[z, x, y, :, 512:640] = jnp.where(lane16 < EXPERTS, high, e16 - high).astype(BF16)

    gathered = (ga, gb, gc)

    def spot(order, k, value, half=None):
        spec = {}
        for axis in order[:k]:
            spec[axis] = pl.ds(0, 4)
        if half is not None:
            spec[order[0]] = pl.ds(2 * half, 2)
        spec[order[k]] = value
        for axis in order[k + 1 :]:
            spec[axis] = at[axis]
        return spec["z"], spec["x"], spec["y"]

    gstate = [None] * 3

    def gather_start(p, k):
        order, ref = GATHER[p], gathered[p]
        a = order[k]
        if k < 2:
            here = ref.at[spot(order, k, at[a])]
            gstate[p] = [go(remote(here, here, near(a, d))) for d in (2, 1, 3)]
            return
        gstate[p] = []
        for half, d in ((0, 1), (1, 3)):
            here = ref.at[spot(order, k, at[a], half)]
            gstate[p].append(go(remote(here, here, near(a, d))))

    def gather_rest(p, k):
        order, ref = GATHER[p], gathered[p]
        a = order[k]
        for half, d in ((1, 1), (0, 3)):
            here = ref.at[spot(order, k, at[a], half)]
            gstate[p].append(go(remote(here, here, near(a, d))))

    def gather_forward(p, k):
        order, ref = GATHER[p], gathered[p]
        a = order[k]
        gstate[p][0].wait_recv()
        one = ref.at[spot(order, k, plus(a, -1), 0)]
        one = go(remote(one, one, near(a, 1)))
        gstate[p][1].wait_recv()
        two = ref.at[spot(order, k, plus(a, 1), 1)]
        two = go(remote(two, two, near(a, 3)))
        gstate[p] = gstate[p][2:] + [one, two]

    def gather_wait(p, n):
        for copy in gstate[p][:n]:
            copy.wait_recv()
        gstate[p] = gstate[p][n:]

    def attend(lo, hi):
        @pl.loop(lo, hi)
        def _(i):
            both = qt[i].T
            qv[i] = jnp.where(role == 0, both[0:64], both[64:128])
            s = jnp.dot(qv[i], cv[i], preferred_element_type=F32)
            s = s * SCORE_SCALE
            live = lax.broadcasted_iota(jnp.int32, (64, 256), 1) < lengths[i]
            s = jnp.where(live, s, -jnp.inf)
            peak = jnp.max(s, axis=1, keepdims=True)
            w = jnp.where(live, jnp.exp(s - peak), 0.0).astype(BF16)
            sums[i] = jnp.broadcast_to(jnp.sum(w.astype(F32), axis=1, keepdims=True), (64, 128))
            peaks[i] = jnp.broadcast_to(peak, (64, 128))
            summed[i] = lax.dot_general(
                w, cv[i, 0:LAT, :], (((1,), (1,)), ((), ())), preferred_element_type=F32
            )

    def gate_up_slice(zz, first=False):
        k = pl.ds(pl.multiple_of(BASE[0] + zz * WIDTH[0], 128), WIDTH[0])

        @pl.loop(0, 2)
        def _(n):
            cols = pl.ds(pl.multiple_of(n * 512, 512), 512)
            rows = ga[zz].reshape(256, WIDTH[0])
            out = jnp.dot(rows, wgu[k, cols], preferred_element_type=F32).reshape(4, 4, 16, 512)
            acc[..., cols] = out if first else acc[..., cols] + out

    def gate_up_rows(*ds):
        for p in (1, 2):
            picks = []
            for d in ds:
                axis = GATHER[p][2]
                picks.append((plus("x", d), slice(None)) if axis == "x" else (slice(None), plus("y", d)))

            @pl.loop(0, 1)
            def _(n, p=p, picks=picks):
                cols = pl.ds(pl.multiple_of(n * 1024, 1024), 1024)
                rows = [
                    jnp.concatenate(
                        [gathered[p][i, a, b, :, 0 : WIDTH[p]].reshape(64, WIDTH[p]) for i in range(4)], axis=1
                    )
                    for a, b in picks
                ]
                rows = jnp.concatenate(rows, axis=0) if len(rows) > 1 else rows[0]
                out = jnp.dot(rows, wgu[pl.ds(BASE[p], 4 * WIDTH[p]), cols], preferred_element_type=F32)
                for i, (a, b) in enumerate(picks):
                    acc[a, b, :, cols] += out[64 * i : 64 * i + 64].reshape(4, 16, 1024)

    for p in range(3):
        gather_start(p, 0)
    load_q.wait()
    load_c.wait()
    attend(0, 4)
    for p in range(3):
        gather_wait(p, 3)
        gather_start(p, 1)
    attend(4, 8)
    store_summed = load(summed, summed_out)
    for p in range(3):
        gather_wait(p, 3)
        gather_start(p, 2)
    for p in range(3):
        gather_rest(p, 2)
    for copy in load_gu:
        copy.wait()
    gate_up_slice(z, True)
    gate_up_rows(0)
    for p in range(3):
        gather_forward(p, 2)
    latent_step(lambda one, two, three, share: [c.wait_recv() for c in one] + [c.start() for c in two])
    for p in range(3):
        gather_wait(p, 2)
    gate_up_slice(plus("z", 1))
    gate_up_slice(plus("z", 3))
    gate_up_rows(1, 3)
    gather_wait(0, 2)
    gate_up_slice(plus("z", 2))
    gather_wait(1, 2)
    gather_wait(2, 2)
    gate_up_rows(2)

    expert = z * 4 + y
    mine = lax.broadcasted_iota(jnp.int32, (256, 128), 1)
    mine = jnp.logical_or(mine == expert, mine == expert + EXPERTS)
    table_all = gc[0, :, :, :, 512:640].reshape(256, 128).astype(F32)
    gate_col[...] = jnp.sum(jnp.where(mine, table_all, 0.0), axis=1, keepdims=True)

    @pl.loop(0, 8)
    def _(i):
        rows = pl.ds(pl.multiple_of(i * 32, 32), 32)
        half = pl.ds(pl.multiple_of(lax.rem(i, 2) * 2, 2), 2)
        g = acc[i // 2, half, :, 0:FFD].reshape(32, FFD)
        u = acc[i // 2, half, :, FFD:].reshape(32, FFD)
        act[rows, :] = (g / (1.0 + jnp.exp(-g)) * u * gate_col[rows, :]).astype(BF16)

    for copy in load_d:
        copy.wait()

    outs = (oa, ob, oc)

    def down(p, zz, n=1):
        k = pl.ds(pl.multiple_of(BASE[p] + zz * WIDTH[p], 128), n * WIDTH[p])
        out = jnp.dot(act[...], wd[:, k], preferred_element_type=F32).astype(BF16)
        for i in range(n):
            outs[p][zz + i] = out[:, i * WIDTH[p] : (i + 1) * WIDTH[p]].reshape(4, 4, 16, WIDTH[p])

    def block(order, s, value, half=None):
        spec = {}
        for axis in order[:s]:
            spec[axis] = pl.ds(0, 1)
        spec[order[s]] = pl.ds(value, 1)
        for axis in order[s + 1 :]:
            spec[axis] = pl.ds(0, 4)
        if half is not None:
            spec[HALVED[SCATTER.index(order)]] = pl.ds(2 * half, 2)
        return spec["z"], spec["x"], spec["y"]

    def part_of(order, half):
        spec = {axis: slice(None) for axis in order}
        spec[HALVED[SCATTER.index(order)]] = pl.ds(2 * half, 2)
        return spec["z"], spec["x"], spec["y"]

    sstate = [[], [], []]

    def scatter_opposite(p, s, cur, half):
        order = SCATTER[p]
        b = order[s]
        to = rs_bufs[p][s][half]
        d = (1, 3)[half]
        sstate[p].append(go(remote(cur.at[block(order, s, plus(b, 2), half)], to, near(b, d))))

    def scatter_direct(p, s, cur):
        order = SCATTER[p]
        b = order[s]
        fl, fr, rl, rr, out = rs_bufs[p][s]
        one = go(remote(cur.at[block(order, s, plus(b, 1), 1)], rl.at[part_of(order, 1)], near(b, 1)))
        two = go(remote(cur.at[block(order, s, plus(b, 3), 0)], rr.at[part_of(order, 0)], near(b, 3)))
        sstate[p] += [one, two]

    def add_into(dst, pieces):
        total = pieces[0].astype(F32)
        for piece in pieces[1:]:
            total = total + piece.astype(F32)
        dst[...] = total.astype(BF16)

    def scatter_forward(p, s, cur):
        order = SCATTER[p]
        b = order[s]
        fl, fr, rl, rr, out = rs_bufs[p][s]
        one, two, three, four = sstate[p]
        one.wait_recv()
        add_into(fl, [fl[...], cur[block(order, s, plus(b, 1), 0)]])
        one = go(remote(fl, rl.at[part_of(order, 0)], near(b, 1)))
        two.wait_recv()
        add_into(fr, [fr[...], cur[block(order, s, plus(b, 3), 1)]])
        two = go(remote(fr, rr.at[part_of(order, 1)], near(b, 3)))
        sstate[p] = [three, four, one, two]

    def scatter_finish(p, s, cur):
        order = SCATTER[p]
        b = order[s]
        fl, fr, rl, rr, out = rs_bufs[p][s]
        for copy in sstate[p]:
            copy.wait_recv()
        add_into(out, [cur[block(order, s, at[b])], rl[...], rr[...]])
        return out

    down(0, plus("z", 2))
    scatter_opposite(0, 0, oa, 0)
    scatter_opposite(0, 0, oa, 1)
    for p in (1, 2):
        for half in (0, 1):
            down(p, 2 * half, 2)
            scatter_opposite(p, 0, outs[p], half)
        scatter_direct(p, 0, outs[p])
    down(0, plus("z", 1))
    down(0, plus("z", 3))
    scatter_direct(0, 0, oa)
    down(0, z)
    cur = list(outs)
    for p in range(3):
        scatter_forward(p, 0, cur[p])
    def scatter_all(p, s):
        order = SCATTER[p]
        b = order[s]
        slots = rs_bufs[p][s][0]
        sstate[p] = [
            go(remote(cur[p].at[block(order, s, plus(b, d))], slots.at[d - 1], near(b, d))) for d in (2, 1, 3)
        ]

    for p in range(3):
        cur[p] = scatter_finish(p, 0, cur[p])
        scatter_all(p, 1)
    latent_step(
        lambda one, two, three, share: [
            two[0].wait_recv(),
            three[0].start(),
            two[1].wait_recv(),
            three[1].start(),
        ]
    )
    for p in range(3):
        order = SCATTER[p]
        slots, out = rs_bufs[p][1]
        for copy in sstate[p]:
            copy.wait_recv()
        add_into(out, [cur[p][block(order, 1, at[order[1]])]] + [slots[d] for d in range(3)])
        cur[p] = out
        scatter_all(p, 2)
    latent_step(lambda one, two, three, share: [c.wait_recv() for c in two[2:] + three] + [share.start()])

    for r, one, two, three, share in latent_plan:

        @pl.when(role == r)
        def _(r=r):
            rows = pl.ds(LOW_ROWS, 112 - LOW_ROWS) if r == 0 else pl.ds(0, LOW_ROWS)
            pltpu.make_async_remote_copy(
                src_ref=wl.at[:, :, rows],
                dst_ref=wl.at[:, :, rows],
                send_sem=send_sems.at[SEND_RING + 9],
                recv_sem=recv_sems.at[share_at],
                device_id=(1 - role, dev),
                device_id_type=MESH,
            ).wait_recv()

    squares = jnp.zeros((16, 1), F32)
    partial = jnp.zeros((16, KVW), F32)
    for p in range(3):
        order = SCATTER[p]
        for copy in sstate[p]:
            copy.wait_recv()
        total = cur[p][block(order, 2, at[order[2]])].reshape(16, WIDTH[p]).astype(F32)
        for d in range(3):
            total = total + rs_bufs[p][2][0][d].reshape(16, WIDTH[p]).astype(F32)
        cols = slice(OFF[p], OFF[p] + WIDTH[p])
        residual = (hid16[:, cols] + total).astype(BF16).astype(F32)
        squares = squares + jnp.sum(jnp.square(residual), axis=1, keepdims=True)
        gain = attn_gain[:, pl.ds(pl.multiple_of(z * SLICE + OFF[p], 128), WIDTH[p])]
        w = wl[...].reshape(SLICE, KVW)[cols]
        partial = partial + jnp.dot((residual * gain).astype(BF16), w, preferred_element_type=F32)
    partial = jnp.concatenate([partial, jnp.broadcast_to(squares, (16, 64))], axis=1)
    for i in range(4):
        tbuf[i] = partial[4 * i : 4 * i + 4]

    last = []
    for d in (2, 1, 3, 0):
        for other in (0, 1):
            if d == 0 and other == 0:
                continue
            to_role = 1 - role if other else role
            last.append(go(remote(tbuf.at[plus("z", d)], ebuf.at[z, role], near("z", d), to_role)))
    ebuf[z, role] = tbuf[z]
    for copy in last:
        copy.wait_recv()
    halves = []
    for r in range(2):
        total = ebuf[0, r]
        for i in range(1, 4):
            total = total + ebuf[i, r]
        halves.append(total)
    comp = jnp.concatenate(halves, axis=0)
    comp = comp[:, 0:KVW] * lax.rsqrt(comp[:, KVW : KVW + 1] / D + EPS)
    content = comp[:, 0:LAT]
    content = content * lax.rsqrt(jnp.mean(jnp.square(content), axis=-1, keepdims=True) + EPS) * kv_gain[...]
    new_latent[:, 0:LAT] = content.astype(BF16)
    new_latent[:, LAT:KVW] = comp[:, LAT:KVW].astype(BF16)

    second = lax.broadcasted_iota(jnp.int32, (64, 128), 1) >= 64
    for i in range(8):
        row = new_latent[i : i + 1, :].astype(F32)
        score = jnp.sum(qv[i].astype(F32) * row, axis=1, keepdims=True) * SCORE_SCALE
        peak_cache = peaks[i][:, 0:1]
        peak = jnp.maximum(peak_cache, score)
        a = jnp.exp(peak_cache - peak)
        b = jnp.exp(score - peak)
        inv = 1.0 / (a * sums[i][:, 0:1] + b)
        factors[i] = jnp.where(second, b * inv, a * inv)

    store_summed.wait()
    assert (count[0], len(loads)) == (COPIES, LOADS - 1), (count[0], len(loads))
    for copy in sent[-SEND_RING:]:
        copy.wait_send()
    latent_step(lambda one, two, three, share: [c.wait_send() for c in one + two + three + [share]])


share_at = 15


def merge(new_latent, factors, summed, latent_out, context):
    latent_out[...] = new_latent[...]
    rows = new_latent[:, 0:LAT].astype(F32)
    rows = jnp.where(pl.program_id(0) == 0, rows[0:4], rows[4:8])
    for i in range(4):
        row = rows[i : i + 1]
        context[i] = (factors[i, :, 0:1] * summed[i] + factors[i, :, 64:65] * row).astype(BF16)


def shards(
    hidden_in,
    expert_ids,
    gate_values,
    ffn_gain,
    w_gate,
    w_up,
    w_down,
    attn_gain,
    w_latent,
    kv_gain,
    queries,
    cache,
    lengths,
):
    vmem = pl.BlockSpec(memory_space=pltpu.VMEM)
    smem = pl.BlockSpec(memory_space=pltpu.SMEM)
    hbm = pl.BlockSpec(memory_space=pl.ANY)
    v = pltpu.VMEM
    scatter_bufs = []
    for p in range(3):
        order, w = SCATTER[p], WIDTH[p]
        stages = []
        shape = [4, 4, 4]
        for s in range(3):
            shape[DIM[order[s]]] = 1
            full = (*shape, 16, w)
            half = list(full)
            half[DIM[HALVED[p]]] = 2
            if s == 0:
                stages.append((v(half, BF16), v(half, BF16), v(full, BF16), v(full, BF16), v(full, BF16)))
            elif s == 1:
                stages.append((v((3, *full), BF16), v(full, BF16)))
            else:
                stages.append((v((3, *full), BF16),))
        scatter_bufs.append(tuple(stages))
    scratch = [
        v((8, D), BF16),
        v((8, 8), jnp.int32),
        v((8, 8), F32),
        v((1, D), F32),
        v((1, D), F32),
        v((1, LAT), F32),
        v((D, 2 * FFD), BF16),
        v((FFD, D), BF16),
        v((4, 4, 112, KVW), BF16),
        v((8, KVW, 128), BF16),
        v((8, 64, KVW), BF16),
        v((8, KVW, 256), BF16),
        v((8, 64, LAT), F32),
        v((8, 64, 128), F32),
        v((8, 64, 128), F32),
        v((4, 4, SLICE), BF16),
        v((4, 128), F32),
        v((4, 4, SLICE), BF16),
        v((4, 4, 128), F32),
        v((16, SLICE), F32),
        v((4, 4, 4, 16, 640), BF16),
        v((4, 4, 4, 16, 640), BF16),
        v((4, 4, 4, 16, 640), BF16),
        v((4, 4, 16, 2 * FFD), F32),
        v((256, 1), F32),
        v((256, FFD), BF16),
        v((4, 4, 4, 16, WIDTH[0]), BF16),
        v((4, 4, 4, 16, WIDTH[1]), BF16),
        v((4, 4, 4, 16, WIDTH[2]), BF16),
        tuple(scatter_bufs),
        v((4, 4, KVW + 64), F32),
        v((4, 2, 4, KVW + 64), F32),
        pltpu.SemaphoreType.DMA((SEND_RING + 10,)),
        pltpu.SemaphoreType.DMA((COPIES,)),
        pltpu.SemaphoreType.DMA((LOADS,)),
    ]
    state = pl.pallas_call(
        kernel,
        out_shape=(
            jax.ShapeDtypeStruct((8, KVW), BF16),
            jax.ShapeDtypeStruct((8, 64, 128), F32),
            jax.ShapeDtypeStruct((8, 64, LAT), F32),
        ),
        in_specs=[hbm] * 6 + [smem] + [hbm] * 6,
        out_specs=(vmem, vmem, hbm),
        scratch_shapes=scratch,
        compiler_params=pltpu.CompilerParams(
            collective_id=0,
            has_side_effects=True,
            vmem_limit_bytes=60 * 1024 * 1024,
        ),
        cost_estimate=pl.CostEstimate(flops=6 * 10**9, bytes_accessed=26 * 10**6, transcendentals=10**6),
    )(
        hidden_in,
        expert_ids,
        gate_values,
        ffn_gain.reshape(1, D),
        attn_gain.reshape(1, D),
        kv_gain.reshape(1, LAT),
        lengths,
        w_gate,
        w_up,
        w_down,
        w_latent,
        jnp.transpose(queries, (0, 2, 1)),
        jnp.transpose(cache, (0, 2, 1)),
    )
    return pl.pallas_call(
        merge,
        grid=(2,),
        out_shape=(
            jax.ShapeDtypeStruct((8, KVW), BF16),
            jax.ShapeDtypeStruct((8, 64, LAT), BF16),
        ),
        in_specs=[
            pl.BlockSpec((8, KVW), lambda i: (0, 0)),
            pl.BlockSpec((4, 64, 128), lambda i: (i, 0, 0)),
            pl.BlockSpec((4, 64, LAT), lambda i: (i, 0, 0)),
        ],
        out_specs=(
            pl.BlockSpec((8, KVW), lambda i: (0, 0)),
            pl.BlockSpec((4, 64, LAT), lambda i: (i, 0, 0)),
        ),
    )(*state)


def solution(mesh):
    in_specs = (
        P("dev", None),
        P("dev", None),
        P("dev", None),
        P(),
        P(None, "dev"),
        P(None, "dev"),
        P("dev", None),
        P(),
        P("dev", None),
        P(),
        P("dev", None, None),
        P("dev", None, None),
        P("dev"),
    )
    out_specs = (P("dev", None), P("dev", "role", None))
    return jax.shard_map(shards, mesh=mesh, in_specs=in_specs, out_specs=out_specs, check_vma=False)
```

```python
import jax
import jax.numpy as jnp
from jax import lax
from jax.experimental import pallas as pl
from jax.experimental.pallas import tpu as pltpu
from jax.sharding import PartitionSpec as P

MESH = pl.DeviceIdType.MESH
F32 = jnp.float32
BF16 = jnp.bfloat16

SCORE_SCALE = 192.0 ** (-0.5)
EPS = 1e-06
D = 7168
SLICE = 1792
FFD = 512
LAT = 512
KVW = 576
EXPERTS = 16
WIDTH = (640, 640, 512)
OFF = (0, 640, 1280)
BASE = (0, 2560, 5120)
GATHER = (("x", "y", "z"), ("y", "z", "x"), ("z", "x", "y"))
SCATTER = tuple(order[::-1] for order in GATHER)
HALVED = ("x", "z", "z")
DIM = {"z": 0, "x": 1, "y": 2}
SEND_RING = 44
COPIES = 101
LOADS = 46
LOW_ROWS = 64


def kernel(
    hidden_in,
    ids_in,
    gates_in,
    ffn_gain_in,
    attn_gain_in,
    kv_gain_in,
    lengths,
    w_gate,
    w_up,
    w_down,
    w_latent,
    queries,
    cache,
    new_latent,
    factors,
    summed_out,
    hidden,
    ids,
    gates,
    ffn_gain,
    attn_gain,
    kv_gain,
    wgu,
    wd,
    wl,
    qt,
    qv,
    cv,
    summed,
    peaks,
    sums,
    xh,
    xe,
    yh,
    ye,
    hid16,
    ga,
    gb,
    gc,
    gx,
    acc,
    gate_col,
    act,
    oa,
    ob,
    oc,
    rs_bufs,
    tbuf,
    ebuf,
    send_sems,
    recv_sems,
    load_sems,
):
    role = lax.axis_index("role")
    dev = lax.axis_index("dev")
    z, y, x = dev // 16, lax.rem(dev // 4, 4), lax.rem(dev, 4)
    at = {"z": z, "y": y, "x": x}
    stride = {"z": 16, "y": 4, "x": 1}

    def plus(axis, d):
        return lax.rem(at[axis] + (d + 4), 4)

    def near(axis, d):
        return dev + (plus(axis, d) - at[axis]) * stride[axis]

    count = [0]
    sent = []

    def remote(src, dst, to_dev, to_role=None, send_at=None):
        i = count[0]
        count[0] += 1
        if send_at is None:
            if len(sent) >= SEND_RING:
                sent[-SEND_RING].wait_send()
            send_at = len(sent) % SEND_RING
        return pltpu.make_async_remote_copy(
            src_ref=src,
            dst_ref=dst,
            send_sem=send_sems.at[send_at],
            recv_sem=recv_sems.at[i],
            device_id=(role if to_role is None else to_role, to_dev),
            device_id_type=MESH,
        )

    def go(copy):
        copy.start()
        sent.append(copy)
        return copy

    loads = []

    def load(src, dst):
        copy = pltpu.make_async_copy(src, dst, load_sems.at[len(loads)])
        copy.start(priority=1)
        loads.append(copy)
        return copy

    barrier = pltpu.get_barrier_semaphore()
    partners = [(role, near(axis, d)) for axis in "xyz" for d in (1, 2, 3)]
    partners += [(1 - role, near("z", d)) for d in (0, 1, 2, 3)]
    for partner in partners:
        pl.semaphore_signal(barrier, inc=1, device_id=partner, device_id_type=MESH)

    small = (
        load(hidden_in, hidden),
        load(ids_in, ids),
        load(gates_in, gates),
        load(ffn_gain_in, ffn_gain),
        load(attn_gain_in, attn_gain),
        load(kv_gain_in, kv_gain),
    )
    load_q = load(queries, qt)
    load_c = load(cache, cv)

    for copy in small:
        copy.wait()
    hid = hidden[...].astype(F32)
    scale = lax.rsqrt(jnp.mean(jnp.square(hid), axis=-1, keepdims=True) + EPS)
    lane = lax.broadcasted_iota(jnp.int32, (8, 128), 1)
    table = jnp.zeros((8, 128), F32)
    for k in range(8):
        table = jnp.where(ids[:, k : k + 1] == lane % EXPERTS, gates[:, k : k + 1], table)
    extra = jnp.where(lane < 2 * EXPERTS, table, scale)
    own = jnp.where(role == 0, hid[0:4], hid[4:8])
    for i in range(4):
        xh[i] = own[:, i * SLICE : (i + 1) * SLICE].astype(BF16)
    xe[...] = jnp.where(role == 0, extra[0:4], extra[4:8])

    pl.semaphore_wait(barrier, len(partners))

    first = []
    for d in (2, 1, 3):
        first.append(go(remote(xh.at[plus("z", d)], yh.at[z], near("z", d))))
        first.append(go(remote(xe, ye.at[z], near("z", d))))

    load_gu, load_d = [], []
    pieces = [(p, i) for p in range(3) for i in range(4)]
    for p, i in pieces:
        here, there = pl.ds(i * SLICE + OFF[p], WIDTH[p]), pl.ds(BASE[p] + i * WIDTH[p], WIDTH[p])
        load_gu.append(load(w_gate.at[here], wgu.at[there, pl.ds(0, FFD)]))
        load_gu.append(load(w_up.at[here], wgu.at[there, pl.ds(FFD, FFD)]))
    def latent_copies():
        out = []
        for r, rows, axes in ((0, pl.ds(0, LOW_ROWS), "xy"), (1, pl.ds(LOW_ROWS, 112 - LOW_ROWS), "yx")):
            a, b = axes
            base = count[0]
            one = [
                remote(
                    wl.at[y, x, rows],
                    wl.at[y, x, rows],
                    near(a, d),
                    send_at=SEND_RING + d - 1,
                )
                for d in (2, 1, 3)
            ]

            def place(pos, half, a=a, rows=rows):
                full = pl.ds(2 * half, 2)
                return wl.at[pos, full, rows] if a == "x" else wl.at[full, pos, rows]

            def send(pos, half, d, k, b=b, place=place):
                return remote(place(pos, half), place(pos, half), near(b, d), send_at=SEND_RING + k)

            two = [send(at[b], 0, 1, 3), send(at[b], 1, 3, 4), send(at[b], 1, 1, 5), send(at[b], 0, 3, 6)]
            three = [send(plus(b, -1), 0, 1, 7), send(plus(b, 1), 1, 3, 8)]
            share = remote(wl.at[:, :, rows], wl.at[:, :, rows], dev, 1 - role, SEND_RING + 9)
            out.append((r, one, two, three, share))
            if r == 0:
                count[0] = base
        return out

    latent_plan = latent_copies()

    def latent_step(action):
        for r, one, two, three, share in latent_plan:

            @pl.when(role == r)
            def _(one=one, two=two, three=three, share=share):
                action(one, two, three, share)

    for r, rows in ((0, pl.ds(0, LOW_ROWS)), (1, pl.ds(LOW_ROWS, 112 - LOW_ROWS))):

        @pl.when(role == r)
        def _(rows=rows):
            own_rows = pltpu.make_async_copy(w_latent.at[rows], wl.at[y, x, rows], load_sems.at[LOADS - 1])
            own_rows.start()
            own_rows.wait()

    latent_step(lambda one, two, three, share: [c.start() for c in one])

    for copy in first:
        copy.wait_recv()
    yh[z] = xh[z]
    ye[z] = xe[...]
    h16 = jnp.concatenate([yh[i].astype(F32) for i in range(4)], axis=0)
    e16 = jnp.concatenate([ye[i] for i in range(4)], axis=0)
    hid16[...] = h16
    col = pl.ds(pl.multiple_of(z * SLICE, 128), SLICE)
    normed = (h16 * e16[:, 2 * EXPERTS : 2 * EXPERTS + 1] * ffn_gain[:, col]).astype(BF16)
    ga[z, x, y] = normed[:, 0:640]
    gb[z, x, y] = normed[:, 640:1280]
    gc[z, x, y] = normed[:, 1280:1792]
    lane16 = lax.broadcasted_iota(jnp.int32, (16, 128), 1)
    high = e16.astype(BF16).astype(F32)
    gx[x, y] = jnp.where(lane16 < EXPERTS, high, e16 - high).astype(BF16)

    gathered = (ga, gb, gc)

    def spot(order, k, value, half=None):
        spec = {}
        for axis in order[:k]:
            spec[axis] = pl.ds(0, 4)
        if half is not None:
            spec[order[0]] = pl.ds(2 * half, 2)
        spec[order[k]] = value
        for axis in order[k + 1 :]:
            spec[axis] = at[axis]
        return spec["z"], spec["x"], spec["y"]

    gstate = [None] * 3

    def gather_start(p, k):
        order, ref = GATHER[p], gathered[p]
        a = order[k]
        if k < 2:
            here = ref.at[spot(order, k, at[a])]
            gstate[p] = [go(remote(here, here, near(a, d))) for d in (2, 1, 3)]
            return
        gstate[p] = []
        for half, d in ((0, 1), (1, 3)):
            here = ref.at[spot(order, k, at[a], half)]
            gstate[p].append(go(remote(here, here, near(a, d))))

    def gather_rest(p, k):
        order, ref = GATHER[p], gathered[p]
        a = order[k]
        for half, d in ((1, 1), (0, 3)):
            here = ref.at[spot(order, k, at[a], half)]
            gstate[p].append(go(remote(here, here, near(a, d))))

    def gather_forward(p, k):
        order, ref = GATHER[p], gathered[p]
        a = order[k]
        gstate[p][0].wait_recv()
        one = ref.at[spot(order, k, plus(a, -1), 0)]
        one = go(remote(one, one, near(a, 1)))
        gstate[p][1].wait_recv()
        two = ref.at[spot(order, k, plus(a, 1), 1)]
        two = go(remote(two, two, near(a, 3)))
        gstate[p] = gstate[p][2:] + [one, two]

    def gather_wait(p, n):
        for copy in gstate[p][:n]:
            copy.wait_recv()
        gstate[p] = gstate[p][n:]

    def attend(lo, hi):
        @pl.loop(lo, hi)
        def _(i):
            both = qt[i].T
            qv[i] = jnp.where(role == 0, both[0:64], both[64:128])
            s = jnp.dot(qv[i], cv[i], preferred_element_type=F32)
            s = s * SCORE_SCALE
            live = lax.broadcasted_iota(jnp.int32, (64, 256), 1) < lengths[i]
            s = jnp.where(live, s, -jnp.inf)
            peak = jnp.max(s, axis=1, keepdims=True)
            w = jnp.where(live, jnp.exp(s - peak), 0.0).astype(BF16)
            sums[i] = jnp.broadcast_to(jnp.sum(w.astype(F32), axis=1, keepdims=True), (64, 128))
            peaks[i] = jnp.broadcast_to(peak, (64, 128))
            summed[i] = lax.dot_general(
                w, cv[i, 0:LAT, :], (((1,), (1,)), ((), ())), preferred_element_type=F32
            )

    def gate_up_slice(zz, first=False):
        k = pl.ds(pl.multiple_of(BASE[0] + zz * WIDTH[0], 128), WIDTH[0])

        rows = ga[zz].reshape(256, WIDTH[0])
        out = jnp.dot(rows, wgu[k, :], preferred_element_type=F32).reshape(4, 4, 16, 2 * FFD)
        acc[...] = out if first else acc[...] + out

    def gate_up_rows(p, *ds):
        picks = []
        for d in ds:
            axis = GATHER[p][2]
            picks.append((plus("x", d), slice(None)) if axis == "x" else (slice(None), plus("y", d)))

        rows = [
            jnp.concatenate([gathered[p][i, a, b].reshape(64, WIDTH[p]) for i in range(4)], axis=1) for a, b in picks
        ]
        rows = jnp.concatenate(rows, axis=0) if len(rows) > 1 else rows[0]
        out = jnp.dot(rows, wgu[pl.ds(BASE[p], 4 * WIDTH[p]), :], preferred_element_type=F32)
        for i, (a, b) in enumerate(picks):
            acc[a, b] += out[64 * i : 64 * i + 64].reshape(4, 16, 2 * FFD)

    def table_start(k):
        here = gx.at[x, y] if k == 0 else gx.at[:, y]
        return [go(remote(here, here, near("xy"[k], d))) for d in (2, 1, 3)]

    for p in range(3):
        gather_start(p, 0)
    table_copies = table_start(0)
    load_q.wait()
    load_c.wait()
    attend(0, 4)
    for p in range(3):
        gather_wait(p, 3)
        gather_start(p, 1)
    for copy in table_copies:
        copy.wait_recv()
    table_copies = table_start(1)
    for p, i in pieces:
        here, there = pl.ds(i * SLICE + OFF[p], WIDTH[p]), pl.ds(BASE[p] + i * WIDTH[p], WIDTH[p])
        load_d.append(load(w_down.at[:, here], wd.at[:, there]))
    attend(4, 8)
    store_summed = load(summed, summed_out)
    for p in range(3):
        gather_wait(p, 3)
        gather_start(p, 2)
    for p in range(3):
        gather_rest(p, 2)
    for copy in load_gu:
        copy.wait()
    gate_up_slice(z, True)
    gate_up_rows(1, 0)
    gate_up_rows(2, 0)
    for p in (2, 0, 1):
        gather_forward(p, 2)
    latent_step(lambda one, two, three, share: [c.wait_recv() for c in one] + [c.start() for c in two])
    gather_wait(2, 2)
    gate_up_rows(2, 1, 3)
    gather_wait(0, 2)
    gate_up_slice(plus("z", 1))
    gate_up_slice(plus("z", 3))
    gather_wait(1, 2)
    gate_up_rows(1, 1, 3)
    gather_wait(2, 2)
    gate_up_rows(2, 2)
    gather_wait(0, 2)
    gate_up_slice(plus("z", 2))
    gather_wait(1, 2)
    gate_up_rows(1, 2)

    for copy in table_copies:
        copy.wait_recv()
    expert = z * 4 + y
    mine = lax.broadcasted_iota(jnp.int32, (256, 128), 1)
    mine = jnp.logical_or(mine == expert, mine == expert + EXPERTS)
    table_all = gx[...].reshape(256, 128).astype(F32)
    gate_col[...] = jnp.sum(jnp.where(mine, table_all, 0.0), axis=1, keepdims=True)

    @pl.loop(0, 4)
    def _(i):
        rows = pl.ds(pl.multiple_of(i * 64, 64), 64)
        g = acc[i, :, :, 0:FFD].reshape(64, FFD)
        u = acc[i, :, :, FFD:].reshape(64, FFD)
        act[rows, :] = (g / (1.0 + jnp.exp(-g)) * u * gate_col[rows, :]).astype(BF16)

    for copy in load_d:
        copy.wait()

    outs = (oa, ob, oc)

    def down(p, zz, n=1):
        k = pl.ds(pl.multiple_of(BASE[p] + zz * WIDTH[p], 128), n * WIDTH[p])
        out = jnp.dot(act[...], wd[:, k], preferred_element_type=F32).astype(BF16)
        for i in range(n):
            outs[p][zz + i] = out[:, i * WIDTH[p] : (i + 1) * WIDTH[p]].reshape(4, 4, 16, WIDTH[p])

    def block(order, s, value, half=None):
        spec = {}
        for axis in order[:s]:
            spec[axis] = pl.ds(0, 1)
        spec[order[s]] = pl.ds(value, 1)
        for axis in order[s + 1 :]:
            spec[axis] = pl.ds(0, 4)
        if half is not None:
            spec[HALVED[SCATTER.index(order)]] = pl.ds(2 * half, 2)
        return spec["z"], spec["x"], spec["y"]

    def part_of(order, half):
        spec = {axis: slice(None) for axis in order}
        spec[HALVED[SCATTER.index(order)]] = pl.ds(2 * half, 2)
        return spec["z"], spec["x"], spec["y"]

    sstate = [[], [], []]

    def scatter_opposite(p, s, cur, half):
        order = SCATTER[p]
        b = order[s]
        to = rs_bufs[p][s][half]
        d = (1, 3)[half]
        sstate[p].append(go(remote(cur.at[block(order, s, plus(b, 2), half)], to, near(b, d))))

    def scatter_direct(p, s, cur):
        order = SCATTER[p]
        b = order[s]
        fl, fr, rl, rr, out = rs_bufs[p][s]
        one = go(remote(cur.at[block(order, s, plus(b, 1), 1)], rl.at[part_of(order, 1)], near(b, 1)))
        two = go(remote(cur.at[block(order, s, plus(b, 3), 0)], rr.at[part_of(order, 0)], near(b, 3)))
        sstate[p] += [one, two]

    def add_into(dst, pieces):
        total = pieces[0].astype(F32)
        for piece in pieces[1:]:
            total = total + piece.astype(F32)
        dst[...] = total.astype(BF16)

    def scatter_forward(p, s, cur):
        order = SCATTER[p]
        b = order[s]
        fl, fr, rl, rr, out = rs_bufs[p][s]
        one, two, three, four = sstate[p]
        one.wait_recv()
        add_into(fl, [fl[...], cur[block(order, s, plus(b, 1), 0)]])
        one = go(remote(fl, rl.at[part_of(order, 0)], near(b, 1)))
        two.wait_recv()
        add_into(fr, [fr[...], cur[block(order, s, plus(b, 3), 1)]])
        two = go(remote(fr, rr.at[part_of(order, 1)], near(b, 3)))
        sstate[p] = [three, four, one, two]

    def scatter_finish(p, s, cur):
        order = SCATTER[p]
        b = order[s]
        fl, fr, rl, rr, out = rs_bufs[p][s]
        for copy in sstate[p]:
            copy.wait_recv()
        add_into(out, [cur[block(order, s, at[b])], rl[...], rr[...]])
        return out

    down(0, plus("z", 2))
    scatter_opposite(0, 0, oa, 0)
    scatter_opposite(0, 0, oa, 1)
    for p in (1, 2):
        for half in (0, 1):
            down(p, 2 * half, 2)
            scatter_opposite(p, 0, outs[p], half)
        scatter_direct(p, 0, outs[p])
    down(0, plus("z", 1))
    down(0, plus("z", 3))
    scatter_direct(0, 0, oa)
    down(0, z)
    cur = list(outs)
    for p in range(3):
        scatter_forward(p, 0, cur[p])
    def scatter_all(p, s):
        order = SCATTER[p]
        b = order[s]
        slots = rs_bufs[p][s][0]
        sstate[p] = [
            go(remote(cur[p].at[block(order, s, plus(b, d))], slots.at[d - 1], near(b, d))) for d in (2, 1, 3)
        ]

    for p in range(3):
        cur[p] = scatter_finish(p, 0, cur[p])
        scatter_all(p, 1)
    latent_step(
        lambda one, two, three, share: [
            two[0].wait_recv(),
            three[0].start(),
            two[1].wait_recv(),
            three[1].start(),
        ]
    )
    for p in range(3):
        order = SCATTER[p]
        slots, out = rs_bufs[p][1]
        for copy in sstate[p]:
            copy.wait_recv()
        add_into(out, [cur[p][block(order, 1, at[order[1]])]] + [slots[d] for d in range(3)])
        cur[p] = out
        scatter_all(p, 2)
    latent_step(lambda one, two, three, share: [c.wait_recv() for c in two[2:] + three] + [share.start()])

    for r, one, two, three, share in latent_plan:

        @pl.when(role == r)
        def _(r=r):
            rows = pl.ds(LOW_ROWS, 112 - LOW_ROWS) if r == 0 else pl.ds(0, LOW_ROWS)
            pltpu.make_async_remote_copy(
                src_ref=wl.at[:, :, rows],
                dst_ref=wl.at[:, :, rows],
                send_sem=send_sems.at[SEND_RING + 9],
                recv_sem=recv_sems.at[share_at],
                device_id=(1 - role, dev),
                device_id_type=MESH,
            ).wait_recv()

    squares = jnp.zeros((16, 1), F32)
    partial = jnp.zeros((16, KVW), F32)
    for p in range(3):
        order = SCATTER[p]
        for copy in sstate[p]:
            copy.wait_recv()
        total = cur[p][block(order, 2, at[order[2]])].reshape(16, WIDTH[p]).astype(F32)
        for d in range(3):
            total = total + rs_bufs[p][2][0][d].reshape(16, WIDTH[p]).astype(F32)
        cols = slice(OFF[p], OFF[p] + WIDTH[p])
        residual = (hid16[:, cols] + total).astype(BF16).astype(F32)
        squares = squares + jnp.sum(jnp.square(residual), axis=1, keepdims=True)
        gain = attn_gain[:, pl.ds(pl.multiple_of(z * SLICE + OFF[p], 128), WIDTH[p])]
        w = wl[...].reshape(SLICE, KVW)[cols]
        partial = partial + jnp.dot((residual * gain).astype(BF16), w, preferred_element_type=F32)
    partial = jnp.concatenate([partial, jnp.broadcast_to(squares, (16, 64))], axis=1)
    for i in range(4):
        tbuf[i] = partial[4 * i : 4 * i + 4]

    last = []
    for d in (2, 1, 3, 0):
        for other in (0, 1):
            if d == 0 and other == 0:
                continue
            to_role = 1 - role if other else role
            last.append(go(remote(tbuf.at[plus("z", d)], ebuf.at[z, role], near("z", d), to_role)))
    ebuf[z, role] = tbuf[z]
    for copy in last:
        copy.wait_recv()
    halves = []
    for r in range(2):
        total = ebuf[0, r]
        for i in range(1, 4):
            total = total + ebuf[i, r]
        halves.append(total)
    comp = jnp.concatenate(halves, axis=0)
    comp = comp[:, 0:KVW] * lax.rsqrt(comp[:, KVW : KVW + 1] / D + EPS)
    content = comp[:, 0:LAT]
    content = content * lax.rsqrt(jnp.mean(jnp.square(content), axis=-1, keepdims=True) + EPS) * kv_gain[...]
    new_latent[:, 0:LAT] = content.astype(BF16)
    new_latent[:, LAT:KVW] = comp[:, LAT:KVW].astype(BF16)

    second = lax.broadcasted_iota(jnp.int32, (64, 128), 1) >= 64
    for i in range(8):
        row = new_latent[i : i + 1, :].astype(F32)
        score = jnp.sum(qv[i].astype(F32) * row, axis=1, keepdims=True) * SCORE_SCALE
        peak_cache = peaks[i][:, 0:1]
        peak = jnp.maximum(peak_cache, score)
        a = jnp.exp(peak_cache - peak)
        b = jnp.exp(score - peak)
        inv = 1.0 / (a * sums[i][:, 0:1] + b)
        factors[i] = jnp.where(second, b * inv, a * inv)

    store_summed.wait()
    assert (count[0], len(loads)) == (COPIES, LOADS - 1), (count[0], len(loads))
    for copy in sent[-SEND_RING:]:
        copy.wait_send()
    latent_step(lambda one, two, three, share: [c.wait_send() for c in one + two + three + [share]])


share_at = 15


def merge(new_latent, factors, summed, latent_out, context):
    latent_out[...] = new_latent[...]
    rows = new_latent[:, 0:LAT].astype(F32)
    for i in range(8):
        row = rows[i : i + 1]
        context[i] = (factors[i, :, 0:1] * summed[i] + factors[i, :, 64:65] * row).astype(BF16)


def shards(
    hidden_in,
    expert_ids,
    gate_values,
    ffn_gain,
    w_gate,
    w_up,
    w_down,
    attn_gain,
    w_latent,
    kv_gain,
    queries,
    cache,
    lengths,
):
    vmem = pl.BlockSpec(memory_space=pltpu.VMEM)
    smem = pl.BlockSpec(memory_space=pltpu.SMEM)
    hbm = pl.BlockSpec(memory_space=pl.ANY)
    v = pltpu.VMEM
    scatter_bufs = []
    for p in range(3):
        order, w = SCATTER[p], WIDTH[p]
        stages = []
        shape = [4, 4, 4]
        for s in range(3):
            shape[DIM[order[s]]] = 1
            full = (*shape, 16, w)
            half = list(full)
            half[DIM[HALVED[p]]] = 2
            if s == 0:
                stages.append((v(half, BF16), v(half, BF16), v(full, BF16), v(full, BF16), v(full, BF16)))
            elif s == 1:
                stages.append((v((3, *full), BF16), v(full, BF16)))
            else:
                stages.append((v((3, *full), BF16),))
        scatter_bufs.append(tuple(stages))
    scratch = [
        v((8, D), BF16),
        v((8, 8), jnp.int32),
        v((8, 8), F32),
        v((1, D), F32),
        v((1, D), F32),
        v((1, LAT), F32),
        v((D, 2 * FFD), BF16),
        v((FFD, D), BF16),
        v((4, 4, 112, KVW), BF16),
        v((8, KVW, 128), BF16),
        v((8, 64, KVW), BF16),
        v((8, KVW, 256), BF16),
        v((8, 64, LAT), F32),
        v((8, 64, 128), F32),
        v((8, 64, 128), F32),
        v((4, 4, SLICE), BF16),
        v((4, 128), F32),
        v((4, 4, SLICE), BF16),
        v((4, 4, 128), F32),
        v((16, SLICE), F32),
        v((4, 4, 4, 16, WIDTH[0]), BF16),
        v((4, 4, 4, 16, WIDTH[1]), BF16),
        v((4, 4, 4, 16, WIDTH[2]), BF16),
        v((4, 4, 16, 128), BF16),
        v((4, 4, 16, 2 * FFD), F32),
        v((256, 1), F32),
        v((256, FFD), BF16),
        v((4, 4, 4, 16, WIDTH[0]), BF16),
        v((4, 4, 4, 16, WIDTH[1]), BF16),
        v((4, 4, 4, 16, WIDTH[2]), BF16),
        tuple(scatter_bufs),
        v((4, 4, KVW + 64), F32),
        v((4, 2, 4, KVW + 64), F32),
        pltpu.SemaphoreType.DMA((SEND_RING + 10,)),
        pltpu.SemaphoreType.DMA((COPIES,)),
        pltpu.SemaphoreType.DMA((LOADS,)),
    ]
    state = pl.pallas_call(
        kernel,
        out_shape=(
            jax.ShapeDtypeStruct((8, KVW), BF16),
            jax.ShapeDtypeStruct((8, 64, 128), F32),
            jax.ShapeDtypeStruct((8, 64, LAT), F32),
        ),
        in_specs=[hbm] * 6 + [smem] + [hbm] * 6,
        out_specs=(vmem, vmem, hbm),
        scratch_shapes=scratch,
        compiler_params=pltpu.CompilerParams(
            collective_id=0,
            has_side_effects=True,
            vmem_limit_bytes=60 * 1024 * 1024,
        ),
        cost_estimate=pl.CostEstimate(flops=6 * 10**9, bytes_accessed=26 * 10**6, transcendentals=10**6),
    )(
        hidden_in,
        expert_ids,
        gate_values,
        ffn_gain.reshape(1, D),
        attn_gain.reshape(1, D),
        kv_gain.reshape(1, LAT),
        lengths,
        w_gate,
        w_up,
        w_down,
        w_latent,
        jnp.transpose(queries, (0, 2, 1)),
        jnp.transpose(cache, (0, 2, 1)),
    )
    return pl.pallas_call(
        merge,
        grid=(1,),
        out_shape=(
            jax.ShapeDtypeStruct((8, KVW), BF16),
            jax.ShapeDtypeStruct((8, 64, LAT), BF16),
        ),
        in_specs=[
            pl.BlockSpec((8, KVW), lambda i: (0, 0)),
            pl.BlockSpec((8, 64, 128), lambda i: (i, 0, 0)),
            pl.BlockSpec((8, 64, LAT), lambda i: (i, 0, 0)),
        ],
        out_specs=(
            pl.BlockSpec((8, KVW), lambda i: (0, 0)),
            pl.BlockSpec((8, 64, LAT), lambda i: (i, 0, 0)),
        ),
    )(*state)


def solution(mesh):
    in_specs = (
        P("dev", None),
        P("dev", None),
        P("dev", None),
        P(),
        P(None, "dev"),
        P(None, "dev"),
        P("dev", None),
        P(),
        P("dev", None),
        P(),
        P("dev", None, None),
        P("dev", None, None),
        P("dev"),
    )
    out_specs = (P("dev", None), P("dev", "role", None))
    return jax.shard_map(shards, mesh=mesh, in_specs=in_specs, out_specs=out_specs, check_vma=False)
```

```python
import jax
import jax.numpy as jnp
from jax import lax
from jax.experimental import pallas as pl
from jax.experimental.pallas import tpu as pltpu
from jax.sharding import PartitionSpec as P

MESH = pl.DeviceIdType.MESH
F32 = jnp.float32
BF16 = jnp.bfloat16

SCORE_SCALE = 192.0 ** (-0.5)
EPS = 1e-06
D = 7168
SLICE = 1792
FFD = 512
LAT = 512
KVW = 576
EXPERTS = 16
WIDTH = (640, 640, 512)
OFF = (0, 640, 1280)
BASE = (0, 2560, 5120)
GATHER = (("x", "y", "z"), ("y", "z", "x"), ("z", "x", "y"))
SCATTER = tuple(order[::-1] for order in GATHER)
HALVED = ("x", "z", "z")
DIM = {"z": 0, "x": 1, "y": 2}
SEND_RING = 44
COPIES = 101
LOADS = 46
LOW_ROWS = 64


def kernel(
    hidden_in,
    ids_in,
    gates_in,
    ffn_gain_in,
    attn_gain_in,
    kv_gain_in,
    lengths,
    w_gate,
    w_up,
    w_down,
    w_latent,
    queries,
    cache,
    new_latent,
    factors,
    summed_out,
    hidden,
    ids,
    gates,
    ffn_gain,
    attn_gain,
    kv_gain,
    wgu,
    wd,
    wl,
    qt,
    qv,
    cv,
    summed,
    peaks,
    sums,
    xh,
    xe,
    yh,
    ye,
    hid16,
    ga,
    gb,
    gc,
    gx,
    acc,
    gate_col,
    act,
    oa,
    ob,
    oc,
    rs_bufs,
    tbuf,
    ebuf,
    send_sems,
    recv_sems,
    load_sems,
):
    role = lax.axis_index("role")
    dev = lax.axis_index("dev")
    z, y, x = dev // 16, lax.rem(dev // 4, 4), lax.rem(dev, 4)
    at = {"z": z, "y": y, "x": x}
    stride = {"z": 16, "y": 4, "x": 1}

    def plus(axis, d):
        return lax.rem(at[axis] + (d + 4), 4)

    def near(axis, d):
        return dev + (plus(axis, d) - at[axis]) * stride[axis]

    count = [0]
    sent = []

    def remote(src, dst, to_dev, to_role=None, send_at=None):
        i = count[0]
        count[0] += 1
        if send_at is None:
            if len(sent) >= SEND_RING:
                sent[-SEND_RING].wait_send()
            send_at = len(sent) % SEND_RING
        return pltpu.make_async_remote_copy(
            src_ref=src,
            dst_ref=dst,
            send_sem=send_sems.at[send_at],
            recv_sem=recv_sems.at[i],
            device_id=(role if to_role is None else to_role, to_dev),
            device_id_type=MESH,
        )

    def go(copy):
        copy.start()
        sent.append(copy)
        return copy

    loads = []

    def load(src, dst):
        copy = pltpu.make_async_copy(src, dst, load_sems.at[len(loads)])
        copy.start(priority=1)
        loads.append(copy)
        return copy

    barrier = pltpu.get_barrier_semaphore()
    partners = [(role, near(axis, d)) for axis in "xyz" for d in (1, 2, 3)]
    partners += [(1 - role, near("z", d)) for d in (0, 1, 2, 3)]
    for partner in partners:
        pl.semaphore_signal(barrier, inc=1, device_id=partner, device_id_type=MESH)

    small = (
        load(hidden_in, hidden),
        load(ids_in, ids),
        load(gates_in, gates),
        load(ffn_gain_in, ffn_gain),
        load(attn_gain_in, attn_gain),
        load(kv_gain_in, kv_gain),
    )
    load_q = load(queries, qt)
    load_c = load(cache, cv)

    for copy in small:
        copy.wait()
    hid = hidden[...].astype(F32)
    scale = lax.rsqrt(jnp.mean(jnp.square(hid), axis=-1, keepdims=True) + EPS)
    lane = lax.broadcasted_iota(jnp.int32, (8, 128), 1)
    table = jnp.zeros((8, 128), F32)
    for k in range(8):
        table = jnp.where(ids[:, k : k + 1] == lane % EXPERTS, gates[:, k : k + 1], table)
    extra = jnp.where(lane < 2 * EXPERTS, table, scale)
    own = jnp.where(role == 0, hid[0:4], hid[4:8])
    for i in range(4):
        xh[i] = own[:, i * SLICE : (i + 1) * SLICE].astype(BF16)
    xe[...] = jnp.where(role == 0, extra[0:4], extra[4:8])

    pl.semaphore_wait(barrier, len(partners))

    first = []
    for d in (2, 1, 3):
        first.append(go(remote(xh.at[plus("z", d)], yh.at[z], near("z", d))))
        first.append(go(remote(xe, ye.at[z], near("z", d))))

    load_gu, load_d = [], []
    pieces = [(p, i) for p in range(3) for i in range(4)]
    for p, i in pieces:
        here, there = pl.ds(i * SLICE + OFF[p], WIDTH[p]), pl.ds(BASE[p] + i * WIDTH[p], WIDTH[p])
        load_gu.append(load(w_gate.at[here], wgu.at[there, pl.ds(0, FFD)]))
        load_gu.append(load(w_up.at[here], wgu.at[there, pl.ds(FFD, FFD)]))
    def latent_copies():
        out = []
        for r, rows, axes in ((0, pl.ds(0, LOW_ROWS), "xy"), (1, pl.ds(LOW_ROWS, 112 - LOW_ROWS), "yx")):
            a, b = axes
            base = count[0]
            one = [
                remote(
                    wl.at[y, x, rows],
                    wl.at[y, x, rows],
                    near(a, d),
                    send_at=SEND_RING + d - 1,
                )
                for d in (2, 1, 3)
            ]

            def place(pos, half, a=a, rows=rows):
                full = pl.ds(2 * half, 2)
                return wl.at[pos, full, rows] if a == "x" else wl.at[full, pos, rows]

            def send(pos, half, d, k, b=b, place=place):
                return remote(place(pos, half), place(pos, half), near(b, d), send_at=SEND_RING + k)

            two = [send(at[b], 0, 1, 3), send(at[b], 1, 3, 4), send(at[b], 1, 1, 5), send(at[b], 0, 3, 6)]
            three = [send(plus(b, -1), 0, 1, 7), send(plus(b, 1), 1, 3, 8)]
            share = remote(wl.at[:, :, rows], wl.at[:, :, rows], dev, 1 - role, SEND_RING + 9)
            out.append((r, one, two, three, share))
            if r == 0:
                count[0] = base
        return out

    latent_plan = latent_copies()

    def latent_step(action):
        for r, one, two, three, share in latent_plan:

            @pl.when(role == r)
            def _(one=one, two=two, three=three, share=share):
                action(one, two, three, share)

    for r, rows in ((0, pl.ds(0, LOW_ROWS)), (1, pl.ds(LOW_ROWS, 112 - LOW_ROWS))):

        @pl.when(role == r)
        def _(rows=rows):
            own_rows = pltpu.make_async_copy(w_latent.at[rows], wl.at[y, x, rows], load_sems.at[LOADS - 1])
            own_rows.start()
            own_rows.wait()

    latent_step(lambda one, two, three, share: [c.start() for c in one])

    for copy in first:
        copy.wait_recv()
    yh[z] = xh[z]
    ye[z] = xe[...]
    h16 = jnp.concatenate([yh[i].astype(F32) for i in range(4)], axis=0)
    e16 = jnp.concatenate([ye[i] for i in range(4)], axis=0)
    hid16[...] = h16
    col = pl.ds(pl.multiple_of(z * SLICE, 128), SLICE)
    normed = (h16 * e16[:, 2 * EXPERTS : 2 * EXPERTS + 1] * ffn_gain[:, col]).astype(BF16)
    ga[z, x, y] = normed[:, 0:640]
    gb[z, x, y] = normed[:, 640:1280]
    gc[z, x, y] = normed[:, 1280:1792]
    lane16 = lax.broadcasted_iota(jnp.int32, (16, 128), 1)
    high = e16.astype(BF16).astype(F32)
    gx[x, y] = jnp.where(lane16 < EXPERTS, high, e16 - high).astype(BF16)

    gathered = (ga, gb, gc)

    def spot(order, k, value, half=None):
        spec = {}
        for axis in order[:k]:
            spec[axis] = pl.ds(0, 4)
        if half is not None:
            spec[order[0]] = pl.ds(2 * half, 2)
        spec[order[k]] = value
        for axis in order[k + 1 :]:
            spec[axis] = at[axis]
        return spec["z"], spec["x"], spec["y"]

    gstate = [None] * 3

    def gather_start(p, k):
        order, ref = GATHER[p], gathered[p]
        a = order[k]
        if k < 2:
            here = ref.at[spot(order, k, at[a])]
            gstate[p] = [go(remote(here, here, near(a, d))) for d in (2, 1, 3)]
            return
        gstate[p] = []
        for half, d in ((0, 1), (1, 3)):
            here = ref.at[spot(order, k, at[a], half)]
            gstate[p].append(go(remote(here, here, near(a, d))))

    def gather_rest(p, k):
        order, ref = GATHER[p], gathered[p]
        a = order[k]
        for half, d in ((1, 1), (0, 3)):
            here = ref.at[spot(order, k, at[a], half)]
            gstate[p].append(go(remote(here, here, near(a, d))))

    def gather_forward(p, k):
        order, ref = GATHER[p], gathered[p]
        a = order[k]
        gstate[p][0].wait_recv()
        one = ref.at[spot(order, k, plus(a, -1), 0)]
        one = go(remote(one, one, near(a, 1)))
        gstate[p][1].wait_recv()
        two = ref.at[spot(order, k, plus(a, 1), 1)]
        two = go(remote(two, two, near(a, 3)))
        gstate[p] = gstate[p][2:] + [one, two]

    def gather_wait(p, n):
        for copy in gstate[p][:n]:
            copy.wait_recv()
        gstate[p] = gstate[p][n:]

    def attend(lo, hi):
        @pl.loop(lo, hi)
        def _(i):
            both = qt[i].T
            qv[i] = jnp.where(role == 0, both[0:64], both[64:128])
            s = jnp.dot(qv[i], cv[i], preferred_element_type=F32)
            s = s * SCORE_SCALE
            live = lax.broadcasted_iota(jnp.int32, (64, 256), 1) < lengths[i]
            s = jnp.where(live, s, -jnp.inf)
            peak = jnp.max(s, axis=1, keepdims=True)
            w = jnp.where(live, jnp.exp(s - peak), 0.0).astype(BF16)
            sums[i] = jnp.broadcast_to(jnp.sum(w.astype(F32), axis=1, keepdims=True), (64, 128))
            peaks[i] = jnp.broadcast_to(peak, (64, 128))
            summed[i] = lax.dot_general(
                w, cv[i, 0:LAT, :], (((1,), (1,)), ((), ())), preferred_element_type=F32
            )

    def gate_up_slice(zz, first=False):
        k = pl.ds(pl.multiple_of(BASE[0] + zz * WIDTH[0], 128), WIDTH[0])

        rows = ga[zz].reshape(256, WIDTH[0])
        out = jnp.dot(rows, wgu[k, :], preferred_element_type=F32).reshape(4, 4, 16, 2 * FFD)
        acc[...] = out if first else acc[...] + out

    def gate_up_rows(p, *ds):
        picks = []
        for d in ds:
            axis = GATHER[p][2]
            picks.append((plus("x", d), slice(None)) if axis == "x" else (slice(None), plus("y", d)))

        rows = [
            jnp.concatenate([gathered[p][i, a, b].reshape(64, WIDTH[p]) for i in range(4)], axis=1) for a, b in picks
        ]
        rows = jnp.concatenate(rows, axis=0) if len(rows) > 1 else rows[0]
        out = jnp.dot(rows, wgu[pl.ds(BASE[p], 4 * WIDTH[p]), :], preferred_element_type=F32)
        for i, (a, b) in enumerate(picks):
            acc[a, b] += out[64 * i : 64 * i + 64].reshape(4, 16, 2 * FFD)

    def table_start(k):
        here = gx.at[x, y] if k == 0 else gx.at[:, y]
        return [go(remote(here, here, near("xy"[k], d))) for d in (2, 1, 3)]

    for p in range(3):
        gather_start(p, 0)
    table_copies = table_start(0)
    load_q.wait()
    load_c.wait()
    attend(0, 4)
    for p in range(3):
        gather_wait(p, 3)
        gather_start(p, 1)
    for copy in table_copies:
        copy.wait_recv()
    table_copies = table_start(1)
    for p, i in pieces:
        here, there = pl.ds(i * SLICE + OFF[p], WIDTH[p]), pl.ds(BASE[p] + i * WIDTH[p], WIDTH[p])
        load_d.append(load(w_down.at[:, here], wd.at[:, there]))
    attend(4, 8)
    store_summed = load(summed, summed_out)
    for p in range(3):
        gather_wait(p, 3)
        gather_start(p, 2)
    for p in range(3):
        gather_rest(p, 2)
    for copy in load_gu:
        copy.wait()
    gate_up_slice(z, True)
    gate_up_rows(1, 0)
    gate_up_rows(2, 0)
    for p in (2, 0, 1):
        gather_forward(p, 2)
    latent_step(lambda one, two, three, share: [c.wait_recv() for c in one] + [c.start() for c in two])
    gather_wait(2, 2)
    gate_up_rows(2, 1, 3)
    gather_wait(0, 2)
    gate_up_slice(plus("z", 1))
    gate_up_slice(plus("z", 3))
    gather_wait(1, 2)
    gate_up_rows(1, 1, 3)
    gather_wait(2, 2)
    gate_up_rows(2, 2)
    gather_wait(0, 2)
    gate_up_slice(plus("z", 2))
    gather_wait(1, 2)
    gate_up_rows(1, 2)

    for copy in table_copies:
        copy.wait_recv()
    expert = z * 4 + y
    mine = lax.broadcasted_iota(jnp.int32, (256, 128), 1)
    mine = jnp.logical_or(mine == expert, mine == expert + EXPERTS)
    table_all = gx[...].reshape(256, 128).astype(F32)
    gate_col[...] = jnp.sum(jnp.where(mine, table_all, 0.0), axis=1, keepdims=True)

    @pl.loop(0, 4)
    def _(i):
        rows = pl.ds(pl.multiple_of(i * 64, 64), 64)
        g = acc[i, :, :, 0:FFD].reshape(64, FFD)
        u = acc[i, :, :, FFD:].reshape(64, FFD)
        act[rows, :] = (g / (1.0 + jnp.exp(-g)) * u * gate_col[rows, :]).astype(BF16)

    for copy in load_d:
        copy.wait()

    outs = (oa, ob, oc)

    def down(p, zz, n=1):
        k = pl.ds(pl.multiple_of(BASE[p] + zz * WIDTH[p], 128), n * WIDTH[p])
        out = jnp.dot(act[...], wd[:, k], preferred_element_type=F32).astype(BF16)
        for i in range(n):
            outs[p][zz + i] = out[:, i * WIDTH[p] : (i + 1) * WIDTH[p]].reshape(4, 4, 16, WIDTH[p])

    def block(order, s, value, half=None):
        spec = {}
        for axis in order[:s]:
            spec[axis] = pl.ds(0, 1)
        spec[order[s]] = pl.ds(value, 1)
        for axis in order[s + 1 :]:
            spec[axis] = pl.ds(0, 4)
        if half is not None:
            spec[HALVED[SCATTER.index(order)]] = pl.ds(2 * half, 2)
        return spec["z"], spec["x"], spec["y"]

    def part_of(order, half):
        spec = {axis: slice(None) for axis in order}
        spec[HALVED[SCATTER.index(order)]] = pl.ds(2 * half, 2)
        return spec["z"], spec["x"], spec["y"]

    sstate = [[], [], []]

    def scatter_opposite(p, s, cur, half):
        order = SCATTER[p]
        b = order[s]
        to = rs_bufs[p][s][half]
        d = (1, 3)[half]
        sstate[p].append(go(remote(cur.at[block(order, s, plus(b, 2), half)], to, near(b, d))))

    def scatter_direct(p, s, cur):
        order = SCATTER[p]
        b = order[s]
        fl, fr, rl, rr, out = rs_bufs[p][s]
        one = go(remote(cur.at[block(order, s, plus(b, 1), 1)], rl.at[part_of(order, 1)], near(b, 1)))
        two = go(remote(cur.at[block(order, s, plus(b, 3), 0)], rr.at[part_of(order, 0)], near(b, 3)))
        sstate[p] += [one, two]

    def add_into(dst, pieces):
        total = pieces[0].astype(F32)
        for piece in pieces[1:]:
            total = total + piece.astype(F32)
        dst[...] = total.astype(BF16)

    def scatter_forward(p, s, cur):
        order = SCATTER[p]
        b = order[s]
        fl, fr, rl, rr, out = rs_bufs[p][s]
        one, two, three, four = sstate[p]
        one.wait_recv()
        add_into(fl, [fl[...], cur[block(order, s, plus(b, 1), 0)]])
        one = go(remote(fl, rl.at[part_of(order, 0)], near(b, 1)))
        two.wait_recv()
        add_into(fr, [fr[...], cur[block(order, s, plus(b, 3), 1)]])
        two = go(remote(fr, rr.at[part_of(order, 1)], near(b, 3)))
        sstate[p] = [three, four, one, two]

    def scatter_finish(p, s, cur):
        order = SCATTER[p]
        b = order[s]
        fl, fr, rl, rr, out = rs_bufs[p][s]
        for copy in sstate[p]:
            copy.wait_recv()
        add_into(out, [cur[block(order, s, at[b])], rl[...], rr[...]])
        return out

    down(0, plus("z", 2))
    scatter_opposite(0, 0, oa, 0)
    scatter_opposite(0, 0, oa, 1)
    for p in (1, 2):
        for half in (0, 1):
            down(p, 2 * half, 2)
            scatter_opposite(p, 0, outs[p], half)
        scatter_direct(p, 0, outs[p])
    down(0, plus("z", 1))
    down(0, plus("z", 3))
    scatter_direct(0, 0, oa)
    cur = list(outs)
    for p in range(3):
        scatter_forward(p, 0, cur[p])
    down(0, z)

    def scatter_all(p, s):
        order = SCATTER[p]
        b = order[s]
        slots = rs_bufs[p][s][0]
        sstate[p] = [
            go(remote(cur[p].at[block(order, s, plus(b, d))], slots.at[d - 1], near(b, d))) for d in (2, 1, 3)
        ]

    for p in range(3):
        cur[p] = scatter_finish(p, 0, cur[p])
        scatter_all(p, 1)
    latent_step(
        lambda one, two, three, share: [
            two[0].wait_recv(),
            three[0].start(),
            two[1].wait_recv(),
            three[1].start(),
        ]
    )
    for p in range(3):
        order = SCATTER[p]
        slots, out = rs_bufs[p][1]
        for copy in sstate[p]:
            copy.wait_recv()
        add_into(out, [cur[p][block(order, 1, at[order[1]])]] + [slots[d] for d in range(3)])
        cur[p] = out
        scatter_all(p, 2)
    latent_step(lambda one, two, three, share: [c.wait_recv() for c in two[2:] + three] + [share.start()])

    for r, one, two, three, share in latent_plan:

        @pl.when(role == r)
        def _(r=r):
            rows = pl.ds(LOW_ROWS, 112 - LOW_ROWS) if r == 0 else pl.ds(0, LOW_ROWS)
            pltpu.make_async_remote_copy(
                src_ref=wl.at[:, :, rows],
                dst_ref=wl.at[:, :, rows],
                send_sem=send_sems.at[SEND_RING + 9],
                recv_sem=recv_sems.at[share_at],
                device_id=(1 - role, dev),
                device_id_type=MESH,
            ).wait_recv()

    squares = jnp.zeros((16, 1), F32)
    partial = jnp.zeros((16, KVW), F32)
    for p in range(3):
        order = SCATTER[p]
        for copy in sstate[p]:
            copy.wait_recv()
        total = cur[p][block(order, 2, at[order[2]])].reshape(16, WIDTH[p]).astype(F32)
        for d in range(3):
            total = total + rs_bufs[p][2][0][d].reshape(16, WIDTH[p]).astype(F32)
        cols = slice(OFF[p], OFF[p] + WIDTH[p])
        residual = (hid16[:, cols] + total).astype(BF16).astype(F32)
        squares = squares + jnp.sum(jnp.square(residual), axis=1, keepdims=True)
        gain = attn_gain[:, pl.ds(pl.multiple_of(z * SLICE + OFF[p], 128), WIDTH[p])]
        w = wl[...].reshape(SLICE, KVW)[cols]
        partial = partial + jnp.dot((residual * gain).astype(BF16), w, preferred_element_type=F32)
    partial = jnp.concatenate([partial, jnp.broadcast_to(squares, (16, 64))], axis=1)
    for i in range(4):
        tbuf[i] = partial[4 * i : 4 * i + 4]

    last = []
    for d in (2, 1, 3, 0):
        for other in (0, 1):
            if d == 0 and other == 0:
                continue
            to_role = 1 - role if other else role
            last.append(go(remote(tbuf.at[plus("z", d)], ebuf.at[z, role], near("z", d), to_role)))
    ebuf[z, role] = tbuf[z]
    for copy in last:
        copy.wait_recv()
    halves = []
    for r in range(2):
        total = ebuf[0, r]
        for i in range(1, 4):
            total = total + ebuf[i, r]
        halves.append(total)
    comp = jnp.concatenate(halves, axis=0)
    comp = comp[:, 0:KVW] * lax.rsqrt(comp[:, KVW : KVW + 1] / D + EPS)
    content = comp[:, 0:LAT]
    content = content * lax.rsqrt(jnp.mean(jnp.square(content), axis=-1, keepdims=True) + EPS) * kv_gain[...]
    new_latent[:, 0:LAT] = content.astype(BF16)
    new_latent[:, LAT:KVW] = comp[:, LAT:KVW].astype(BF16)

    second = lax.broadcasted_iota(jnp.int32, (64, 128), 1) >= 64
    for i in range(8):
        row = new_latent[i : i + 1, :].astype(F32)
        score = jnp.sum(qv[i].astype(F32) * row, axis=1, keepdims=True) * SCORE_SCALE
        peak_cache = peaks[i][:, 0:1]
        peak = jnp.maximum(peak_cache, score)
        a = jnp.exp(peak_cache - peak)
        b = jnp.exp(score - peak)
        inv = 1.0 / (a * sums[i][:, 0:1] + b)
        factors[i] = jnp.where(second, b * inv, a * inv)

    store_summed.wait()
    assert (count[0], len(loads)) == (COPIES, LOADS - 1), (count[0], len(loads))
    for copy in sent[-SEND_RING:]:
        copy.wait_send()
    latent_step(lambda one, two, three, share: [c.wait_send() for c in one + two + three + [share]])


share_at = 15


def merge(new_latent, factors, summed, latent_out, context):
    latent_out[...] = new_latent[...]
    rows = new_latent[:, 0:LAT].astype(F32)
    for i in range(8):
        row = rows[i : i + 1]
        context[i] = (factors[i, :, 0:1] * summed[i] + factors[i, :, 64:65] * row).astype(BF16)


def shards(
    hidden_in,
    expert_ids,
    gate_values,
    ffn_gain,
    w_gate,
    w_up,
    w_down,
    attn_gain,
    w_latent,
    kv_gain,
    queries,
    cache,
    lengths,
):
    vmem = pl.BlockSpec(memory_space=pltpu.VMEM)
    smem = pl.BlockSpec(memory_space=pltpu.SMEM)
    hbm = pl.BlockSpec(memory_space=pl.ANY)
    v = pltpu.VMEM
    scatter_bufs = []
    for p in range(3):
        order, w = SCATTER[p], WIDTH[p]
        stages = []
        shape = [4, 4, 4]
        for s in range(3):
            shape[DIM[order[s]]] = 1
            full = (*shape, 16, w)
            half = list(full)
            half[DIM[HALVED[p]]] = 2
            if s == 0:
                stages.append((v(half, BF16), v(half, BF16), v(full, BF16), v(full, BF16), v(full, BF16)))
            elif s == 1:
                stages.append((v((3, *full), BF16), v(full, BF16)))
            else:
                stages.append((v((3, *full), BF16),))
        scatter_bufs.append(tuple(stages))
    scratch = [
        v((8, D), BF16),
        v((8, 8), jnp.int32),
        v((8, 8), F32),
        v((1, D), F32),
        v((1, D), F32),
        v((1, LAT), F32),
        v((D, 2 * FFD), BF16),
        v((FFD, D), BF16),
        v((4, 4, 112, KVW), BF16),
        v((8, KVW, 128), BF16),
        v((8, 64, KVW), BF16),
        v((8, KVW, 256), BF16),
        v((8, 64, LAT), F32),
        v((8, 64, 128), F32),
        v((8, 64, 128), F32),
        v((4, 4, SLICE), BF16),
        v((4, 128), F32),
        v((4, 4, SLICE), BF16),
        v((4, 4, 128), F32),
        v((16, SLICE), F32),
        v((4, 4, 4, 16, WIDTH[0]), BF16),
        v((4, 4, 4, 16, WIDTH[1]), BF16),
        v((4, 4, 4, 16, WIDTH[2]), BF16),
        v((4, 4, 16, 128), BF16),
        v((4, 4, 16, 2 * FFD), F32),
        v((256, 1), F32),
        v((256, FFD), BF16),
        v((4, 4, 4, 16, WIDTH[0]), BF16),
        v((4, 4, 4, 16, WIDTH[1]), BF16),
        v((4, 4, 4, 16, WIDTH[2]), BF16),
        tuple(scatter_bufs),
        v((4, 4, KVW + 64), F32),
        v((4, 2, 4, KVW + 64), F32),
        pltpu.SemaphoreType.DMA((SEND_RING + 10,)),
        pltpu.SemaphoreType.DMA((COPIES,)),
        pltpu.SemaphoreType.DMA((LOADS,)),
    ]
    state = pl.pallas_call(
        kernel,
        out_shape=(
            jax.ShapeDtypeStruct((8, KVW), BF16),
            jax.ShapeDtypeStruct((8, 64, 128), F32),
            jax.ShapeDtypeStruct((8, 64, LAT), F32),
        ),
        in_specs=[hbm] * 6 + [smem] + [hbm] * 6,
        out_specs=(vmem, vmem, hbm),
        scratch_shapes=scratch,
        compiler_params=pltpu.CompilerParams(
            collective_id=0,
            has_side_effects=True,
            vmem_limit_bytes=60 * 1024 * 1024,
        ),
        cost_estimate=pl.CostEstimate(flops=6 * 10**9, bytes_accessed=26 * 10**6, transcendentals=10**6),
    )(
        hidden_in,
        expert_ids,
        gate_values,
        ffn_gain.reshape(1, D),
        attn_gain.reshape(1, D),
        kv_gain.reshape(1, LAT),
        lengths,
        w_gate,
        w_up,
        w_down,
        w_latent,
        jnp.transpose(queries, (0, 2, 1)),
        jnp.transpose(cache, (0, 2, 1)),
    )
    return pl.pallas_call(
        merge,
        grid=(1,),
        out_shape=(
            jax.ShapeDtypeStruct((8, KVW), BF16),
            jax.ShapeDtypeStruct((8, 64, LAT), BF16),
        ),
        in_specs=[
            pl.BlockSpec((8, KVW), lambda i: (0, 0)),
            pl.BlockSpec((8, 64, 128), lambda i: (i, 0, 0)),
            pl.BlockSpec((8, 64, LAT), lambda i: (i, 0, 0)),
        ],
        out_specs=(
            pl.BlockSpec((8, KVW), lambda i: (0, 0)),
            pl.BlockSpec((8, 64, LAT), lambda i: (i, 0, 0)),
        ),
    )(*state)


def solution(mesh):
    in_specs = (
        P("dev", None),
        P("dev", None),
        P("dev", None),
        P(),
        P(None, "dev"),
        P(None, "dev"),
        P("dev", None),
        P(),
        P("dev", None),
        P(),
        P("dev", None, None),
        P("dev", None, None),
        P("dev"),
    )
    out_specs = (P("dev", None), P("dev", "role", None))
    return jax.shard_map(shards, mesh=mesh, in_specs=in_specs, out_specs=out_specs, check_vma=False)
```
